128 devices in a mesh: gx: 8 (over x, core), gy: 16 (over z, y).
Axes of the slice: x: 4, y: 4, z: 4, core: 2. Of those that a mesh axis runs over, the one named last changes fastest.
Arguments:
- previous_fine_boxes: float32 [1024, 5, 8, 128], P(('gx', 'gy'))
- coarse_state: float32 [5, 128, 8192], P(None, 'gx', 'gy')
- new_source: int32 [1024], replicated, may hold values from 0 to 1023, as said below
- box_position: int32 [1024], replicated, may hold values from 0 to 4095, as said below
Outputs:
- fine_boxes: float32 [1024, 5, 8, 128], P(('gx', 'gy'))
- reflux: float32 [4096, 5, 136], P(('gx', 'gy'))
The draws below stay inside these ranges and needn't reach their ends.
Inputs may be any that keep to these rules, and one draw needn't show every extreme that they name: `new_source`: a permutation; the old slot of every new slot lies on a device of the same gx index; of the 8 new slots of a device, 4 hold its own old boxes and each other device of its gx group sends it either 0 or exactly 1 boxes. `box_position`: positions of the boxes are distinct; the coarse owner of a box's position lies in the gx group of the box's new owner; the boxes of one new owner lie in either 0 or exactly 2 positions of each coarse device.
All inputs are finite; a program needn't handle non-finite values.
Results may differ from the reference program's by a relative error of at most 0.0003.
Values sent between devices are 32-bit elements; how exact they have to be, the bound alone decides.
A program may use at most 64 MiB of HBM per device.

```python
import jax
import jax.numpy as jnp
from jax import lax

FX = 8
FY = 128
PXD = 4
PYD = 8
POS_DEV = 32
BOX_DEV = 8
MOVE_CAP = 1
BOXES = 1024
POSITIONS = 4096
NCX = 128
NCY = 8192
N_GX = 8
N_GY = 16


GAMMA_LESS = 0.4


def choose_shifts(subkey, members, peer_count):
    values = jnp.arange(1, members, dtype=jnp.int32)
    fixed = (values == 1) | (values == members - 1) | (values == members // 2)
    scores = jax.random.permutation(subkey, members - 1).astype(jnp.int32) + members * fixed.astype(jnp.int32)
    picked = lax.top_k(scores, peer_count)[1]
    return values[picked]


def layout(key):
    boxes_here = BOX_DEV
    members = N_GY
    groups = N_GX
    per_peer = MOVE_CAP
    peer_count = boxes_here // (2 * per_peer)
    devices_all = groups * members
    keys = jax.random.split(key, 6)
    shuffle = jax.vmap(lambda subkey: jax.random.permutation(subkey, boxes_here))(jax.random.split(keys[0], devices_all))
    shifts = jax.vmap(lambda subkey: choose_shifts(subkey, members, peer_count))(jax.random.split(keys[1], groups))
    slot_ids = jnp.arange(boxes_here)
    pair_ids = jnp.clip((slot_ids - boxes_here // 2) // per_peer, 0, peer_count - 1)
    step_sizes = shifts[:, pair_ids]
    member_ids = jnp.arange(members)
    sender_gy = jnp.where(slot_ids[None, None, :] < boxes_here // 2, member_ids[None, :, None], (member_ids[None, :, None] + step_sizes[:, None, :]) % members)
    sender_dev = jnp.arange(groups)[:, None, None] * members + sender_gy
    sender_local = shuffle[sender_dev, jnp.broadcast_to(slot_ids[None, None, :], sender_dev.shape)]
    sources = (sender_dev * boxes_here + sender_local).reshape(devices_all, boxes_here)
    reorder = jax.vmap(lambda subkey: jax.random.permutation(subkey, boxes_here))(jax.random.split(keys[2], devices_all))
    new_map = jnp.take_along_axis(sources, reorder, axis=1).reshape(-1).astype(jnp.int32)
    scores = jax.random.randint(keys[3], (groups, members, members), 0, 4 * members)
    hot_start = jax.random.randint(keys[4], (groups,), 0, members)
    hot_cells = ((member_ids[None, :] - hot_start[:, None]) % members < max(members // 4, 1)).astype(jnp.int32)
    scores = (scores + 3 * members * hot_cells[:, None, :]) * members + member_ids[None, None, :]
    chosen = lax.top_k(scores, boxes_here // 2)[1]
    box_coarse = chosen[:, :, slot_ids // 2].reshape(groups, members * boxes_here)
    one_hot = (box_coarse[:, :, None] == member_ids[None, None, :]).astype(jnp.int32)
    before = jnp.cumsum(one_hot, axis=1) - one_hot
    ranks = jnp.sum(before * one_hot, axis=2)
    place_perm = jax.vmap(lambda subkey: jax.random.permutation(subkey, POS_DEV))(jax.random.split(keys[5], devices_all))
    coarse_dev = jnp.arange(groups)[:, None] * members + box_coarse
    local_position_index = place_perm[coarse_dev, ranks]
    positions = (coarse_dev * POS_DEV + local_position_index).reshape(-1).astype(jnp.int32)
    placed = jnp.zeros((devices_all * boxes_here,), jnp.int32).at[new_map].set(positions)
    return (new_map, placed)


def draw_new_source(key, part):
    return layout(key)[0]


def draw_box_position(key, part):
    return layout(key)[1]


def euler_state(key, shape, dens_low, dens_high, swirl, spread):
    keys = jax.random.split(key, 5)
    density = jax.random.uniform(keys[0], shape, jnp.float32, dens_low, dens_high)
    velocity_horizontal = swirl * jax.random.truncated_normal(keys[1], -3.0, 3.0, shape, jnp.float32)
    speed_y = swirl * jax.random.truncated_normal(keys[2], -3.0, 3.0, shape, jnp.float32)
    speed_z = 0.5 * swirl * jax.random.truncated_normal(keys[3], -3.0, 3.0, shape, jnp.float32)
    pressure = jax.random.uniform(keys[4], shape, jnp.float32, 1.0 - spread, 1.0 + spread)
    energy = pressure / GAMMA_LESS + 0.5 * density * (velocity_horizontal * velocity_horizontal + speed_y * speed_y + speed_z * speed_z)
    return jnp.stack([density, density * velocity_horizontal, density * speed_y, density * speed_z, energy], axis=-3)


def draw_previous_fine_boxes(key, part):
    key = jax.random.fold_in(key, 5)
    return euler_state(key, (BOXES, FX, FY), 1.0, 2.0, 0.5, 0.4)


def draw_coarse_state(key, part):
    key = jax.random.fold_in(key, 9)
    return euler_state(key, (NCX, NCY), 1.0, 2.0, 0.5, 0.4)


def setup_inputs(seed: int = 0) -> dict:
    arg_keys = jax.random.split(jax.random.key(seed), 5)
    return {
        "previous_fine_boxes": draw_previous_fine_boxes(jax.random.fold_in(arg_keys[4], 71), 0),
        "coarse_state": draw_coarse_state(jax.random.fold_in(arg_keys[4], 71), 0),
        "new_source": draw_new_source(jax.random.fold_in(arg_keys[4], 71), 0),
        "box_position": draw_box_position(jax.random.fold_in(arg_keys[4], 71), 0),
    }


GAMMA_LESS = 0.4
STEP_RATIO = 0.15
WAVE_SPEED = 2.5


def minmod(first, second):
    return jnp.where(first * second > 0.0, jnp.where(jnp.abs(first) < jnp.abs(second), first, second), 0.0)


def physical_flux(state, along_dim):
    inverse = 1.0 / state[0]
    pressure = GAMMA_LESS * (state[4] - 0.5 * (state[1] * state[1] + state[2] * state[2] + state[3] * state[3]) * inverse)
    normal = state[along_dim] * inverse
    pieces = [state[along_dim], state[1] * normal, state[2] * normal, state[3] * normal, (state[4] + pressure) * normal]
    pieces[along_dim] = pieces[along_dim] + pressure
    return jnp.stack(pieces)


def boundary_face_flux(state, along_dim):
    length = state.shape[along_dim]

    def window(start_at, stop_at, source):
        return lax.slice_in_dim(source, start_at, stop_at, axis=along_dim)

    deltas = window(1, length, state) - window(0, length - 1, state)
    limited = minmod(window(0, length - 2, deltas), window(1, length - 1, deltas))
    left_state = window(1, length - 2, state) + 0.5 * window(0, length - 3, limited)
    right_state = window(2, length - 1, state) - 0.5 * window(1, length - 2, limited)
    average = 0.5 * (physical_flux(left_state, along_dim) + physical_flux(right_state, along_dim))
    return average - 0.5 * WAVE_SPEED * (right_state - left_state)


def advance(state):
    x_flux = boundary_face_flux(state, 1)
    y_flux = boundary_face_flux(state, 2)
    inner = state[:, 2:-2, 2:-2]
    result = inner - STEP_RATIO * (x_flux[:, 1:, 2:-2] - x_flux[:, :-1, 2:-2]) - STEP_RATIO * (y_flux[:, 2:-2, 1:] - y_flux[:, 2:-2, :-1])
    return result, x_flux, y_flux


def pair_sum(values):
    return values.reshape(values.shape[0], values.shape[1] // 2, 2).sum(axis=2)


def face_sums(x_flux, y_flux, margin, box_rows, box_cols):
    x_lower = x_flux[:, margin - 2, margin:margin + box_cols]
    x_upper = x_flux[:, margin + box_rows - 2, margin:margin + box_cols]
    y_lower = y_flux[:, margin:margin + box_rows, margin - 2]
    y_upper = y_flux[:, margin:margin + box_rows, margin + box_cols - 2]
    return jnp.concatenate([pair_sum(x_lower), pair_sum(x_upper), pair_sum(y_lower), pair_sum(y_upper)], axis=1)


def prolong(coarse_block):
    center = coarse_block[:, 1:-1, 1:-1]
    slope_x = minmod(center - coarse_block[:, :-2, 1:-1], coarse_block[:, 2:, 1:-1] - center)
    slope_y = minmod(center - coarse_block[:, 1:-1, :-2], coarse_block[:, 1:-1, 2:] - center)
    offsets = jnp.array([-0.25, 0.25], jnp.float32)
    refined = (center[:, :, None, :, None]
               + slope_x[:, :, None, :, None] * offsets[None, None, :, None, None]
               + slope_y[:, :, None, :, None] * offsets[None, None, None, None, :])
    return refined.reshape(coarse_block.shape[0], 2 * center.shape[1], 2 * center.shape[2])


def advance_twice(padded, box_rows, box_cols):
    middle, x_flux, y_flux = advance(padded)
    totals = face_sums(x_flux, y_flux, 4, box_rows, box_cols)
    result, x_flux, y_flux = advance(middle)
    return result, totals + face_sums(x_flux, y_flux, 2, box_rows, box_cols)


def coarse_faces(coarse_block, half_rows, half_cols):
    x_lower = boundary_face_flux(coarse_block[:, 1:5, 3:3 + half_cols], 1)[:, 0]
    x_upper = boundary_face_flux(coarse_block[:, half_rows + 1:half_rows + 5, 3:3 + half_cols], 1)[:, 0]
    y_lower = boundary_face_flux(coarse_block[:, 3:3 + half_rows, 1:5], 2)[:, :, 0]
    y_upper = boundary_face_flux(coarse_block[:, 3:3 + half_rows, half_cols + 1:half_cols + 5], 2)[:, :, 0]
    return jnp.concatenate([x_lower, x_upper, y_lower, y_upper], axis=1)


def face_signs(half_rows, half_cols):
    return jnp.concatenate([jnp.ones((half_cols,), jnp.float32), -jnp.ones((half_cols,), jnp.float32),
                            jnp.ones((half_rows,), jnp.float32), -jnp.ones((half_rows,), jnp.float32)])


def reference(previous_fine_boxes, coarse_state, new_source, box_position):
    box_rows = previous_fine_boxes.shape[2]
    box_cols = previous_fine_boxes.shape[3]
    half_rows = box_rows // 2
    half_cols = box_cols // 2
    padded_coarse = jnp.pad(coarse_state, ((0, 0), (3, 3), (3, 3)), mode="wrap")
    signs = face_signs(half_rows, half_cols)

    def update(slot_id):
        source = new_source[slot_id]
        position = box_position[source]
        owner = position // POS_DEV
        within = position % POS_DEV
        row_start = (owner // N_GY) * (PXD * half_rows) + (within // PYD) * half_rows
        col_start = (owner % N_GY) * (PYD * half_cols) + (within % PYD) * half_cols
        zero_index = jnp.zeros((), jnp.int32)
        coarse_block = lax.dynamic_slice(padded_coarse, (zero_index, row_start.astype(jnp.int32), col_start.astype(jnp.int32)),
                                         (5, half_rows + 6, half_cols + 6))
        padded = prolong(coarse_block).at[:, 4:-4, 4:-4].set(previous_fine_boxes[source])
        result, totals = advance_twice(padded, box_rows, box_cols)
        coarse_terms = STEP_RATIO * coarse_faces(coarse_block, half_rows, half_cols)
        flux_corrections = signs * (coarse_terms - 0.25 * STEP_RATIO * totals)
        return result, flux_corrections, position

    fine_boxes, flux_corrections, positions = lax.map(update, jnp.arange(previous_fine_boxes.shape[0], dtype=jnp.int32))
    reflux = jnp.zeros((POSITIONS, 5, box_rows + box_cols), jnp.float32).at[positions].set(flux_corrections)
    return fine_boxes, reflux
```

```python
import jax
import jax.numpy as jnp
from jax import lax
from jax.experimental import pallas as pl
from jax.experimental.pallas import tpu as pltpu
from jax.sharding import PartitionSpec as P

MESH = pl.DeviceIdType.MESH
F32 = jnp.float32
I32 = jnp.int32

GROUP = 16
SLABS = 8
GAMMA_LESS = 0.4
STEP_RATIO = 0.15
WAVE_SPEED = 2.5
HALF_STEP = 0.5 * STEP_RATIO
SUM_SCALE = 0.25 * STEP_RATIO * 0.5

T_DEV, T_LOC, T_OWN, T_RANK, T_BOX, T_POS, T_BACK, T_INV = 0, 1, 2, 3, 4, 5, 7, 9


def iota(axis):
    return lax.broadcasted_iota(I32, (8, 128), axis)


def shift_lanes(x, by):
    by = by % 128
    return x if by == 0 else pltpu.roll(x, by, axis=1)


def pick_lanes(x, index):
    return jnp.take_along_axis(x, index, axis=1)


def minmod(a, b):
    return jnp.maximum(jnp.minimum(a, b), 0.0) + jnp.minimum(jnp.maximum(a, b), 0.0)


def scaled_flux(state, along, sign):
    rho, m1, m2, m3, energy = state
    inverse = 1.0 / rho
    pressure = GAMMA_LESS * (energy - 0.5 * (m1 * m1 + m2 * m2 + m3 * m3) * inverse)
    normal = state[along] * inverse
    pieces = [state[along], m1 * normal, m2 * normal, m3 * normal, (energy + pressure) * normal]
    pieces[along] = pieces[along] + pressure
    speed = sign * WAVE_SPEED
    return [p + speed * u for p, u in zip(pieces, state)]


def cell_sides(low, mid, high, along):
    half = [0.5 * minmod(m - l, h - m) for l, m, h in zip(low, mid, high)]
    lower = scaled_flux([m - s for m, s in zip(mid, half)], along, -1.0)
    upper = scaled_flux([m + s for m, s in zip(mid, half)], along, 1.0)
    return lower, upper


def interface_flux(cells, along):
    a, b, c, d = cells
    left = [y + 0.5 * minmod(y - x, z - y) for x, y, z in zip(a, b, c)]
    right = [y - 0.5 * minmod(y - x, z - y) for x, y, z in zip(b, c, d)]
    upper = scaled_flux(left, along, 1.0)
    lower = scaled_flux(right, along, -1.0)
    return [u + l for u, l in zip(upper, lower)]


def make_tables(src_ref, pos_ref, gx, me, table):
    lane = iota(1)
    sub = iota(0)
    src = jnp.broadcast_to(src_ref[pl.ds(gx, 1), :], (8, 128)) & 127
    pos = jnp.broadcast_to(pos_ref[pl.ds(gx, 1), :], (8, 128)) & 511
    place = pick_lanes(pos, src)
    device = src >> 3
    local = src & 7
    owner = place >> 5
    spot = place & 31
    within = lane & 7
    group = lane >> 3
    rank = jnp.zeros((8, 128), I32)
    for d in range(1, 8):
        rank = rank + jnp.where((within >= d) & (shift_lanes(owner, d) == owner), 1, 0)

    def group_sum(v):
        for d in (1, 2, 4):
            v = v + shift_lanes(v, -d)
        return v

    mine = 8 * me + within
    my_owner = pick_lanes(owner, mine)
    my_rank = pick_lanes(rank, mine)
    rows = [device, local, owner, rank, group_sum(jnp.where(device == me, local, 0)) & 7]
    for a in range(2):
        rows.append(group_sum(jnp.where((owner == me) & (rank == a), spot, 0)) & 31)
    for a in range(2):
        rows.append(group_sum(jnp.where((my_owner == group) & (my_rank == a), within, 0)) & 7)
    inverse = jnp.zeros((8, 128), I32)
    for block in range(4):
        number = sub + 8 * block
        v = jnp.where((owner == me) & (spot == number), group * 2 + rank + 1, 0)
        for d in (64, 32, 16, 8, 4, 2, 1):
            v = v + shift_lanes(v, d)
        inverse = inverse + jnp.where(lane == number, v, 0)
    for d in (4, 2, 1):
        inverse = inverse + pltpu.roll(inverse, d, axis=0)
    rows.append(jnp.minimum(inverse, 32))
    for i, row in enumerate(rows):
        table[pl.ds(i, 1), :] = row[0:1, :]


def body(
    boxes, coarse, src_ref, pos_ref, fine_out, reflux_out,
    table, tabs, rim, strips, rows_x, cols_x, halo_send, halo_recv, edge_recv,
    box_send, box_recv, ghost_send, ghost_recv, sum_send, sum_recv,
    mixed, turned, coarse_c, coarse_s, state_a, state_b, low_y, high_y, faces_x, faces_y,
    back, fine_buf, sums_x, sums_y, line_x, line_y, own_x, own_y, out_x, out_y,
    table_sem, out_sem, halo_ss, halo_rs, box_ss, box_rs, ghost_ss, ghost_rs, sum_ss, sum_rs,
):
    gx = lax.axis_index("gx")
    me = lax.axis_index("gy")
    lane = iota(1)
    sub = iota(0)

    def peer(o):
        return lax.rem(me + o, GROUP)

    def slab(o):
        return lax.rem(gx + o + SLABS, SLABS)

    near = [(slab(1), me), (slab(-1), me)]
    corner = [(slab(dx), lax.rem(me + dy + GROUP, GROUP)) for dy in (-1, 1) for dx in (-1, 0, 1)]
    barrier = pltpu.get_barrier_semaphore()
    for o in range(1, GROUP):
        pl.semaphore_signal(barrier, inc=1, device_id=(gx, peer(o)), device_id_type=MESH)
    others = near + [corner[0], corner[2], corner[3], corner[5]]
    for there in others:
        pl.semaphore_signal(barrier, inc=1, device_id=there, device_id_type=MESH)

    make_tables(src_ref, pos_ref, gx, me, table)
    to_scalars = pltpu.make_async_copy(table, tabs, table_sem)
    to_scalars.start()

    for t in range(4):
        for f in range(5):
            tile = coarse[f, :, t * 128 : t * 128 + 128]
            halo_send[0, t, 3 * f : 3 * f + 3] = tile[13:16]
            halo_send[1, t, 3 * f : 3 * f + 3] = tile[0:3]
            rim[t * 5 + f, 8:24] = tile
            rim[20 + t * 5 + f, 8:24] = pltpu.roll(tile, 64, axis=1)
            rows_x[t, 22 * f + 3 : 22 * f + 19] = tile
    strips[0] = rows_x[0].T[0:8]
    strips[1] = rows_x[3].T[120:128]

    pl.semaphore_wait(barrier, GROUP - 1 + len(others))
    halo_copies = []
    for i, there in enumerate(near):
        halo_copies.append(
            pltpu.make_async_remote_copy(
                halo_send.at[i], halo_recv.at[i], halo_ss.at[i], halo_rs.at[i], there, MESH
            )
        )
    for i, there in enumerate(corner):
        halo_copies.append(
            pltpu.make_async_remote_copy(
                strips.at[i // 3], edge_recv.at[i], halo_ss.at[2 + i], halo_rs.at[2 + i], there, MESH
            )
        )
    for copy in halo_copies:
        copy.start()

    to_scalars.wait()

    def box_copy(o):
        return pltpu.make_async_remote_copy(
            box_send.at[o], box_recv.at[me], box_ss.at[o], box_rs.at[o], (gx, peer(o)), MESH
        )

    def ghost_copy(o):
        return pltpu.make_async_remote_copy(
            ghost_send.at[o], ghost_recv.at[me], ghost_ss.at[o], ghost_rs.at[o], (gx, peer(o)), MESH
        )

    def sum_copy(o):
        return pltpu.make_async_remote_copy(
            sum_send.at[o], sum_recv.at[me], sum_ss.at[o], sum_rs.at[o], (gx, peer(o)), MESH
        )

    def send_box(o, carry):
        which = tabs[T_BOX, 8 * peer(o)] & 7
        box_send[o] = boxes[which]
        box_copy(o).start()
        return carry

    lax.fori_loop(1, GROUP, send_box, 0)

    for copy in halo_copies:
        copy.wait_recv()
    for t in range(4):
        for f in range(5):
            top = halo_recv[0, t, 3 * f : 3 * f + 3]
            bottom = halo_recv[1, t, 3 * f : 3 * f + 3]
            rim[t * 5 + f, 5:8] = top
            rim[t * 5 + f, 24:27] = bottom
            rim[20 + t * 5 + f, 5:8] = pltpu.roll(top, 64, axis=1)
            rim[20 + t * 5 + f, 24:27] = pltpu.roll(bottom, 64, axis=1)
            rows_x[t, 22 * f : 22 * f + 3] = top
            rows_x[t, 22 * f + 19 : 22 * f + 22] = bottom
    for t in range(4):
        cols_x[8 + 128 * t : 136 + 128 * t] = rows_x[t].T
    field = jnp.zeros((8, 128), I32)
    for f in range(1, 5):
        field = field + jnp.where(lane >= 22 * f, 1, 0)
    place = lane - 22 * field
    for side, base in ((1, 0), (0, 520)):
        own = edge_recv[3 * side + 1]
        top = shift_lanes(edge_recv[3 * side + 2], -16)
        bottom = shift_lanes(edge_recv[3 * side], 16)
        cols_x[base : base + 8] = jnp.where(place < 3, top, jnp.where(place >= 19, bottom, own))

    first_lane = lane < 64
    top_rows = sub < 4
    tenth = jnp.zeros((8, 128), I32)
    for i in range(1, 12):
        tenth = tenth + jnp.where(lane >= 10 * i, 1, 0)
    side_index = jnp.where(lane < 100, 22 * jnp.where(tenth >= 5, tenth - 5, tenth) + lane - 10 * tenth, 0)

    def pack_ghosts(o, dest, slot):
        at = 8 * peer(o)
        spots = [tabs[T_POS, at] & 31, tabs[T_POS + 1, at] & 31]
        rs = [s >> 3 for s in spots]
        cs = [s & 7 for s in spots]
        ids = [(((c & 1) ^ a) * 4 + (c >> 1)) * 5 for a, c in enumerate(cs)]
        for f in range(5):
            parts = [
                jnp.where(
                    top_rows, rim[ids[a] + f, pl.ds(4 * rs[a] + 5, 8), :], rim[ids[a] + f, pl.ds(4 * rs[a] + 7, 8), :]
                )
                for a in range(2)
            ]
            dest[slot, f] = jnp.where(first_lane, parts[0], parts[1])
        sides = []
        for a in range(2):
            strip = jnp.where(
                top_rows, cols_x[pl.ds(64 * cs[a] + 5, 8), :], cols_x[pl.ds(64 * cs[a] + 67, 8), :]
            )
            sides.append(pick_lanes(strip, side_index + 4 * rs[a]))
        dest[slot, 5] = jnp.where(lane < 50, sides[0], sides[1])

    def send_ghosts(o, carry):
        pack_ghosts(o, ghost_send, o)
        ghost_copy(o).start()
        return carry

    lax.fori_loop(1, GROUP, send_ghosts, 0)
    pack_ghosts(0, ghost_recv, me)

    scale_x = jnp.where(first_lane, HALF_STEP, -HALF_STEP)
    for t in range(4):
        cells = [
            [rim[t * 5 + f, pl.ds(8 + k, 8, stride=4), :] for f in range(5)] for k in (-2, -1, 0, 1)
        ]
        flux = interface_flux(cells, 1)
        for f in range(5):
            line_x[t, pl.ds(f, 8, stride=8), :] = flux[f]
    for f5 in range(2):
        cells = [
            [
                shift_lanes(cols_x[pl.ds(8 + k + 512 * f5, 8, stride=64), :], -(22 * f + 3))
                for f in range(5)
            ]
            for k in (-2, -1, 0, 1)
        ]
        flux = interface_flux(cells, 2)
        for f in range(5):
            line_y[pl.ds(64 * f5 + f, 8, stride=8), :] = flux[f]
    scale_y = jnp.where(lane < 4, HALF_STEP, -HALF_STEP)
    for r in range(4):
        for t in range(4):
            low = line_x[t, 8 * r : 8 * r + 8]
            high = line_x[t, 8 * r + 8 : 8 * r + 16]
            own_x[8 * r + 2 * t] = scale_x * jnp.where(first_lane, low, shift_lanes(high, 64))
            own_x[8 * r + 2 * t + 1] = scale_x * jnp.where(first_lane, shift_lanes(low, 64), high)
        for c in range(8):
            low = line_y[8 * c : 8 * c + 8]
            high = line_y[8 * c + 8 : 8 * c + 16]
            own_y[8 * r + c] = scale_y * jnp.where(
                lane < 4, shift_lanes(low, -4 * r), shift_lanes(high, 4 - 4 * r)
            )

    def wait_boxes(o, carry):
        box_copy(o).wait_recv()
        return carry

    def wait_ghosts(o, carry):
        ghost_copy(o).wait_recv()
        return carry

    lax.fori_loop(1, GROUP, wait_boxes, 0)
    lax.fori_loop(1, GROUP, wait_ghosts, 0)
    side_parts = [jnp.zeros((8, 128), F32) for _ in range(5)]
    for b in range(8):
        at = 8 * me + b
        device = tabs[T_DEV, at] & 15
        local = tabs[T_LOC, at] & 7
        owner = tabs[T_OWN, at] & 15
        second = tabs[T_RANK, at] == 1
        stays = device == me
        for f in range(5):
            box = jnp.where(stays, boxes[local, f], box_recv[device, f])
            inner = ghost_recv[owner, f]
            inner = jnp.where(second, shift_lanes(inner, 64), inner)
            mixed[f, 16 * b : 16 * b + 8] = inner
            mixed[f, 16 * b + 8 : 16 * b + 16] = box
        side = ghost_recv[owner, 5]
        side = jnp.where(second, shift_lanes(side, -50), side)
        for f in range(5):
            side_parts[f] = jnp.where((lane >> 4) == b, shift_lanes(side, 16 * b - 10 * f), side_parts[f])

    ring = (lane - 4) & 127
    row = ring & 15
    base = ring - row
    coarse_row = (row >> 1) + 1

    def kept(i):
        return jnp.where(i < 4, i, jnp.where(i < 6, 3, i - 2))

    inner_index = [base + kept(coarse_row + d) for d in (0, -1, 1)]
    side_rows = [base + coarse_row + d for d in (0, -1, 1)]
    interior = (lane & 8) != 0
    row_sign = jnp.where((row & 1) == 0, -0.25, 0.25)
    for f in range(5):
        turned[f] = mixed[f].T
        for k in range(8):
            block = turned[f, 8 * k : 8 * k + 8]
            mid, low, high = [pick_lanes(block, index) for index in inner_index]
            coarse_c[f, 3 + 8 * k : 11 + 8 * k] = mid
            coarse_s[f, 3 + 8 * k : 11 + 8 * k] = row_sign * minmod(mid - low, high - mid)
        mid, low, high = [pick_lanes(side_parts[f], index) for index in side_rows]
        slope = row_sign * minmod(mid - low, high - mid)
        coarse_c[f, 0:4] = mid[0:4]
        coarse_c[f, 66:70] = mid[4:8]
        coarse_s[f, 0:4] = slope[0:4]
        coarse_s[f, 66:70] = slope[4:8]
        for k in range(9):
            j = 1 + 8 * k
            mid = coarse_c[f, j : j + 8]
            slope = minmod(mid - coarse_c[f, j - 1 : j + 7], coarse_c[f, j + 1 : j + 9] - mid)
            middle = mid + coarse_s[f, j : j + 8]
            state_a[f, pl.ds(2 * j - 2, 8, stride=2), :] = middle - 0.25 * slope
            state_a[f, pl.ds(2 * j - 1, 8, stride=2), :] = middle + 0.25 * slope
        for k in range(16):
            m = 4 + 8 * k
            state_a[f, m : m + 8] = jnp.where(interior, turned[f, 8 * k : 8 * k + 8], state_a[f, m : m + 8])

    lower_face = (lane & 15) == 7

    def step(state, result, last):
        def chunk(k, carry):
            m = pl.multiple_of(8 * k, 8)
            mid = [state[f, pl.ds(m + 1, 8), :] for f in range(5)]
            low = [state[f, pl.ds(m, 8), :] for f in range(5)]
            high = [state[f, pl.ds(m + 2, 8), :] for f in range(5)]
            lower, upper = cell_sides(low, mid, high, 2)
            for f in range(5):
                low_y[f, pl.ds(m + 9, 8), :] = lower[f]
                high_y[f, pl.ds(m + 9, 8), :] = upper[f]
            cells = low
            lower, upper = cell_sides(
                [shift_lanes(u, 1) for u in cells], cells, [shift_lanes(u, -1) for u in cells], 1
            )
            for f in range(5):
                after = upper[f] + shift_lanes(lower[f], -1)
                before = shift_lanes(upper[f], 1) + lower[f]
                after_y = high_y[f, pl.ds(m + 8, 8), :] + low_y[f, pl.ds(m + 9, 8), :]
                before_y = high_y[f, pl.ds(m + 7, 8), :] + low_y[f, pl.ds(m + 8, 8), :]
                new = cells[f] - HALF_STEP * (after - before) - HALF_STEP * (after_y - before_y)
                face = jnp.where(lower_face, after, before)
                if last:
                    face = face + faces_x[f, pl.ds(m, 8), :]
                    result[f, pl.ds(m, 8), :] = jnp.where(interior, new, face)
                else:
                    faces_x[f, pl.ds(m, 8), :] = face
                    result[f, pl.ds(m, 8), :] = new
            return carry

        lax.fori_loop(0, 17, chunk, 0)
        for f in range(5):
            for i, m in enumerate((3, 131)):
                flux = high_y[f, m + 8 : m + 9] + low_y[f, m + 9 : m + 10]
                if last:
                    flux = flux + faces_y[i, f : f + 1]
                faces_y[i, f : f + 1] = flux

    step(state_a, state_b, False)
    step(state_b, state_a, True)

    pair_index = 2 * (lane & 63)
    for f in range(5):
        back[f, 0:128] = state_a[f, 4:132].T
        back[f, 128:136] = back[f, 0:8]
        for b in range(8):
            fine_buf[b, f] = back[f, 16 * b + 8 : 16 * b + 16]
        low = back[f, pl.ds(7, 8, stride=16), :]
        high = back[f, pl.ds(16, 8, stride=16), :]
        low = low + shift_lanes(low, -1)
        high = high + shift_lanes(high, -1)
        sums_x[pl.ds(f, 8, stride=8), :] = jnp.where(
            first_lane, pick_lanes(low, pair_index), pick_lanes(high, pair_index)
        )
    to_fine = pltpu.make_async_copy(fine_buf, fine_out, out_sem)
    low = faces_y[0] + shift_lanes(faces_y[0], -1)
    high = faces_y[1] + shift_lanes(faces_y[1], -1)
    for b in range(8):
        index = 16 * b + 8 + 2 * (lane & 3)
        sums_y[b] = jnp.where((lane & 4) == 0, pick_lanes(low, index), pick_lanes(high, index))

    def pack_sums(o, dest, slot):
        at = 8 * peer(o)
        first = tabs[T_BACK, at] & 7
        second = tabs[T_BACK + 1, at] & 7
        dest[slot, 0:8] = sums_x[pl.ds(8 * first, 8), :]
        dest[slot, 5:13] = sums_x[pl.ds(8 * second, 8), :]
        dest[slot, 10:16] = jnp.where(lane < 8, sums_y[first], sums_y[second])[0:6]

    def send_sums(o, carry):
        pack_sums(o, sum_send, o)
        sum_copy(o).start()
        return carry

    def wait_sums(o, carry):
        sum_copy(o).wait_recv()
        return carry

    lax.fori_loop(1, GROUP, send_sums, 0)
    pack_sums(0, sum_recv, me)
    to_fine.start()

    for copy in halo_copies:
        copy.wait_send()

    def wait_sent(o, carry):
        box_copy(o).wait_send()
        ghost_copy(o).wait_send()
        return carry

    lax.fori_loop(1, GROUP, wait_sent, 0)
    lax.fori_loop(1, GROUP, wait_sums, 0)

    sign_x = jnp.where(first_lane, SUM_SCALE, -SUM_SCALE)
    for n in range(32):
        entry = tabs[T_INV, n]
        live = entry > 0
        slot = (entry - 1) & 31
        sender = slot >> 1
        second = (slot & 1) == 1
        total_x = sum_recv[sender, pl.ds(5 * (slot & 1), 8), :]
        total_y = sum_recv[sender, pl.ds(10, 6), :]
        total_y = jnp.where(second, pltpu.roll(total_y, 120, axis=1), total_y)
        sign_y = jnp.where(lane[0:5] < 4, SUM_SCALE, -SUM_SCALE)
        out_x[pl.ds(n, 5, stride=32), :] = jnp.where(live, own_x[n, 0:5] - sign_x[0:5] * total_x[0:5], 0.0)
        out_y[pl.ds(n, 5, stride=32), :] = jnp.where(live, own_y[n, 0:5] - sign_y * total_y[0:5], 0.0)
    for f in range(5):
        reflux_out[f, :, 0:128] = out_x[32 * f : 32 * f + 32]
        reflux_out[f, :, 128:136] = out_y[32 * f : 32 * f + 32][:, 0:8]

    def wait_sums_sent(o, carry):
        sum_copy(o).wait_send()
        return carry

    lax.fori_loop(1, GROUP, wait_sums_sent, 0)
    to_fine.wait()


def local(previous_fine_boxes, coarse_state, new_source, box_position):
    vmem = pl.BlockSpec(memory_space=pltpu.VMEM)
    dma = pltpu.SemaphoreType.DMA
    v = pltpu.VMEM
    fine, reflux = pl.pallas_call(
        body,
        out_shape=(
            jax.ShapeDtypeStruct((8, 5, 8, 128), F32),
            jax.ShapeDtypeStruct((5, 32, 136), F32),
        ),
        in_specs=[vmem] * 4,
        out_specs=(pl.BlockSpec(memory_space=pl.ANY), vmem),
        scratch_shapes=[
            v((16, 128), I32),
            pltpu.SMEM((16, 128), I32),
            v((40, 48, 128), F32),
            v((2, 8, 128), F32),
            v((4, 128, 128), F32),
            v((1040, 128), F32),
            v((2, 4, 16, 128), F32),
            v((2, 4, 16, 128), F32),
            v((6, 8, 128), F32),
            v((16, 5, 8, 128), F32),
            v((16, 5, 8, 128), F32),
            v((16, 6, 8, 128), F32),
            v((16, 6, 8, 128), F32),
            v((16, 16, 128), F32),
            v((16, 16, 128), F32),
            v((5, 128, 128), F32),
            v((5, 128, 128), F32),
            v((5, 80, 128), F32),
            v((5, 80, 128), F32),
            v((5, 152, 128), F32),
            v((5, 152, 128), F32),
            v((5, 160, 128), F32),
            v((5, 160, 128), F32),
            v((5, 136, 128), F32),
            v((2, 8, 128), F32),
            v((5, 144, 128), F32),
            v((8, 5, 8, 128), F32),
            v((72, 128), F32),
            v((8, 8, 128), F32),
            v((4, 72, 128), F32),
            v((136, 128), F32),
            v((32, 8, 128), F32),
            v((32, 8, 128), F32),
            v((192, 128), F32),
            v((192, 128), F32),
            dma,
            dma,
            dma((8,)),
            dma((8,)),
            dma((16,)),
            dma((16,)),
            dma((16,)),
            dma((16,)),
            dma((16,)),
            dma((16,)),
        ],
        compiler_params=pltpu.CompilerParams(
            collective_id=0, has_side_effects=True, vmem_limit_bytes=40 * 1024 * 1024
        ),
    )(
        previous_fine_boxes,
        coarse_state,
        new_source.reshape(8, 128),
        box_position.reshape(8, 128),
    )
    return fine, jnp.transpose(reflux, (1, 0, 2))


def solution(mesh):
    placed = (P(("gx", "gy"), None, None, None), P(None, "gx", "gy"), P(), P())
    return jax.shard_map(
        local,
        mesh=mesh,
        in_specs=placed,
        out_specs=(P(("gx", "gy"), None, None, None), P(("gx", "gy"), None, None)),
        check_vma=False,
    )
```

```python
import jax
import jax.numpy as jnp
from jax import lax
from jax.experimental import pallas as pl
from jax.experimental.pallas import tpu as pltpu
from jax.sharding import PartitionSpec as P

MESH = pl.DeviceIdType.MESH
F32 = jnp.float32
I32 = jnp.int32

GROUP = 16
SLABS = 8
GAMMA_LESS = 0.4
STEP_RATIO = 0.15
WAVE_SPEED = 2.5
HALF_STEP = 0.5 * STEP_RATIO
SUM_SCALE = 0.25 * STEP_RATIO * 0.5

T_DEV, T_LOC, T_OWN, T_RANK, T_SPOT, T_BOX, T_INV = 0, 1, 2, 3, 4, 5, 6
T_POS, T_POS_NEXT, T_POS_BEFORE, T_BACK = 8, 10, 12, 14


def iota(axis):
    return lax.broadcasted_iota(I32, (8, 128), axis)


def shift_lanes(x, by):
    by = by % 128
    return x if by == 0 else pltpu.roll(x, by, axis=1)


def pick_lanes(x, index):
    return jnp.take_along_axis(x, index, axis=1)


def minmod(a, b):
    return jnp.maximum(jnp.minimum(a, b), jnp.minimum(jnp.maximum(a, b), 0.0))


def scaled_flux(state, along, sign):
    rho, m1, m2, m3, energy = state
    speed = sign * WAVE_SPEED
    inverse = 1.0 / rho
    pressure = GAMMA_LESS * (energy - 0.5 * (m1 * m1 + m2 * m2 + m3 * m3) * inverse)
    normal = state[along] * inverse
    moved = normal + speed
    pieces = [
        state[along] + speed * rho, m1 * moved, m2 * moved, m3 * moved, energy * moved + pressure * normal
    ]
    pieces[along] = pieces[along] + pressure
    return pieces


def cell_sides(low, mid, high, along):
    half = [0.5 * minmod(m - l, h - m) for l, m, h in zip(low, mid, high)]
    lower = scaled_flux([m - s for m, s in zip(mid, half)], along, -1.0)
    upper = scaled_flux([m + s for m, s in zip(mid, half)], along, 1.0)
    return lower, upper


def interface_flux(cells, along):
    a, b, c, d = cells
    left = [y + 0.5 * minmod(y - x, z - y) for x, y, z in zip(a, b, c)]
    right = [y - 0.5 * minmod(y - x, z - y) for x, y, z in zip(b, c, d)]
    upper = scaled_flux(left, along, 1.0)
    lower = scaled_flux(right, along, -1.0)
    return [u + l for u, l in zip(upper, lower)]


def make_tables(src_ref, pos_ref, gx, me, table):
    lane = iota(1)
    sub = iota(0)
    src = jnp.broadcast_to(src_ref[pl.ds(gx, 1), :], (8, 128)) & 127
    pos = jnp.broadcast_to(pos_ref[pl.ds(gx, 1), :], (8, 128)) & 511
    place = pick_lanes(pos, src)
    device = src >> 3
    local = src & 7
    owner = place >> 5
    spot = place & 31
    within = lane & 7
    group = lane >> 3
    rank = jnp.zeros((8, 128), I32)
    for d in range(1, 8):
        rank = rank + jnp.where((within >= d) & (shift_lanes(owner, d) == owner), 1, 0)

    def group_sum(v):
        for d in (1, 2, 4):
            v = v + shift_lanes(v, -d)
        return v

    mine = 8 * me + within
    my_owner = pick_lanes(owner, mine)
    my_rank = pick_lanes(rank, mine)
    after = (me + 1) & 15
    before = (me + 15) & 15
    rows = [device, local, owner, rank, spot, group_sum(jnp.where(device == me, local, 0)) & 7]
    inverse = jnp.zeros((8, 128), I32)
    for block in range(4):
        number = sub + 8 * block
        v = jnp.where((owner == me) & (spot == number), group * 2 + rank + 1, 0)
        for d in (64, 32, 16, 8, 4, 2, 1):
            v = v + shift_lanes(v, d)
        inverse = inverse + jnp.where(lane == number, v, 0)
    for d in (4, 2, 1):
        inverse = inverse + pltpu.roll(inverse, d, axis=0)
    rows += [jnp.minimum(inverse, 32), rank]
    for whose in (me, after, before):
        for a in range(2):
            rows.append(group_sum(jnp.where((owner == whose) & (rank == a), spot, 0)) & 31)
    for a in range(2):
        rows.append(group_sum(jnp.where((my_owner == group) & (my_rank == a), within, 0)) & 7)
    for i, row in enumerate(rows):
        table[pl.ds(i, 1), :] = row[0:1, :]


def body(
    boxes_in, coarse_in, src_in, pos_in, fine_out, reflux_out,
    boxes, coarse, src_ref, pos_ref, table, tabs, rim, rows_x, cols_x, halo_send, halo_recv, edge_recv,
    box_send, box_recv, ghost_send, ghost_recv, sum_send, sum_recv,
    mixed, turned, coarse_c, coarse_s, state_a, state_b, low_y, high_y, low_x, high_x, change_x, faces_x, faces_y,
    face_cols, face_rows, back, sums_x, sums_y, line_x, line_y, own_x, own_y, out_x, out_y,
    table_sem, in_sem, halo_ss, halo_rs, box_ss, box_rs, ghost_ss, ghost_rs, sum_ss, sum_rs,
):
    gx = lax.axis_index("gx")
    me = lax.axis_index("gy")
    lane = iota(1)
    sub = iota(0)

    def peer(o):
        return lax.rem(me + o, GROUP)

    def slab(o):
        return lax.rem(gx + o + SLABS, SLABS)

    near = [(slab(1), me), (slab(-1), me)]
    beside = [(gx, peer(GROUP - 1)), (gx, peer(1))]
    barrier = pltpu.get_barrier_semaphore()
    for there in near:
        pl.semaphore_signal(barrier, inc=1, device_id=there, device_id_type=MESH)
    for o in (1, 15, 4, 12, 2, 14, 8, 3, 13, 5, 11, 6, 10, 7, 9):
        pl.semaphore_signal(barrier, inc=1, device_id=(gx, peer(o)), device_id_type=MESH)
    fetches = [
        pltpu.make_async_copy(coarse_in, coarse, in_sem.at[0]),
        pltpu.make_async_copy(src_in, src_ref, in_sem.at[1]),
        pltpu.make_async_copy(pos_in, pos_ref, in_sem.at[2]),
        pltpu.make_async_copy(boxes_in, boxes, in_sem.at[3]),
    ]
    for fetch in fetches:
        fetch.start()

    fetches[1].wait()
    fetches[2].wait()
    make_tables(src_ref, pos_ref, gx, me, table)
    to_scalars = pltpu.make_async_copy(table, tabs, table_sem)
    to_scalars.start()

    fetches[0].wait()
    for t in range(4):
        for f in range(5):
            tile = coarse[f, :, t * 128 : t * 128 + 128]
            halo_send[0, t, 3 * f : 3 * f + 3] = tile[13:16]
            halo_send[1, t, 3 * f : 3 * f + 3] = tile[0:3]
            rim[t * 5 + f, 8:24] = tile
            rim[20 + t * 5 + f, 8:24] = pltpu.roll(tile, 64, axis=1)
            rows_x[t, 22 * f + 3 : 22 * f + 19] = tile

    pl.semaphore_wait(barrier, GROUP + 1)
    halo_copies = []
    for i, there in enumerate(near):
        halo_copies.append(
            pltpu.make_async_remote_copy(
                halo_send.at[i], halo_recv.at[i], halo_ss.at[i], halo_rs.at[i], there, MESH
            )
        )
    for copy in halo_copies:
        copy.start()

    to_scalars.wait()
    fetches[3].wait()

    def box_copy(o):
        return pltpu.make_async_remote_copy(
            box_send.at[o], box_recv.at[me], box_ss.at[o], box_rs.at[o], (gx, peer(o)), MESH
        )

    def ghost_copy(o):
        return pltpu.make_async_remote_copy(
            ghost_send.at[o], ghost_recv.at[me], ghost_ss.at[o], ghost_rs.at[o], (gx, peer(o)), MESH
        )

    def sum_copy(o):
        return pltpu.make_async_remote_copy(
            sum_send.at[o], sum_recv.at[me], sum_ss.at[o], sum_rs.at[o], (gx, peer(o)), MESH
        )

    def send_box(o, carry):
        which = tabs[T_BOX, 8 * peer(o)] & 7
        box_send[o] = boxes[which]
        box_copy(o).start()
        return carry

    lax.fori_loop(1, GROUP, send_box, 0)

    for copy in halo_copies:
        copy.wait_recv()
    for t in range(4):
        for f in range(5):
            top = halo_recv[0, t, 3 * f : 3 * f + 3]
            bottom = halo_recv[1, t, 3 * f : 3 * f + 3]
            rim[t * 5 + f, 5:8] = top
            rim[t * 5 + f, 24:27] = bottom
            rim[20 + t * 5 + f, 5:8] = pltpu.roll(top, 64, axis=1)
            rim[20 + t * 5 + f, 24:27] = pltpu.roll(bottom, 64, axis=1)
            rows_x[t, 22 * f : 22 * f + 3] = top
            rows_x[t, 22 * f + 19 : 22 * f + 22] = bottom
    for t in range(4):
        cols_x[8 + 128 * t : 136 + 128 * t] = rows_x[t].T
    edge_copies = [
        pltpu.make_async_remote_copy(
            cols_x.at[pl.ds(at, 8)], edge_recv.at[i], halo_ss.at[2 + i], halo_rs.at[2 + i], there, MESH
        )
        for i, (at, there) in enumerate(zip((8, 512), beside))
    ]
    for copy in edge_copies:
        copy.start()

    first_lane = lane < 64
    top_rows = sub < 4
    tenth = jnp.zeros((8, 128), I32)
    for i in range(1, 12):
        tenth = tenth + jnp.where(lane >= 10 * i, 1, 0)
    side_index = jnp.where(lane < 100, 22 * jnp.where(tenth >= 5, tenth - 5, tenth) + lane - 10 * tenth, 0)

    def pack_ghosts(o, dest, slot):
        at = 8 * peer(o)
        spots = [tabs[T_POS, at] & 31, tabs[T_POS + 1, at] & 31]
        rs = [s >> 3 for s in spots]
        cs = [s & 7 for s in spots]
        ids = [(((c & 1) ^ a) * 4 + (c >> 1)) * 5 for a, c in enumerate(cs)]
        for f in range(5):
            parts = [
                jnp.where(
                    top_rows, rim[ids[a] + f, pl.ds(4 * rs[a] + 5, 8), :], rim[ids[a] + f, pl.ds(4 * rs[a] + 7, 8), :]
                )
                for a in range(2)
            ]
            dest[slot, f] = jnp.where(first_lane, parts[0], parts[1])
        sides = []
        for a in range(2):
            strip = jnp.where(
                top_rows, cols_x[pl.ds(64 * cs[a] + 5, 8), :], cols_x[pl.ds(64 * cs[a] + 67, 8), :]
            )
            sides.append(pick_lanes(strip, side_index + 4 * rs[a]))
        dest[slot, 5] = jnp.where(lane < 50, sides[0], sides[1])
        edge = jnp.where(top_rows, cols_x[517:525], cols_x[3:11])
        edges = []
        for a in range(2):
            low = (tabs[T_POS_NEXT + a, at] & 31) >> 3
            high = (tabs[T_POS_BEFORE + a, at] & 31) >> 3
            edges.append(pick_lanes(edge, side_index + 4 * jnp.where(top_rows, low, high)))
        dest[slot, 6] = jnp.where(lane < 50, edges[0], edges[1])

    def send_ghosts(o, carry):
        pack_ghosts(o, ghost_send, o)
        ghost_copy(o).start()
        return carry

    lax.fori_loop(1, GROUP, send_ghosts, 0)
    pack_ghosts(0, ghost_recv, me)

    scale_x = jnp.where(first_lane, HALF_STEP, -HALF_STEP)
    for t in range(4):
        cells = [
            [rim[t * 5 + f, pl.ds(8 + k, 8, stride=4), :] for f in range(5)] for k in (-2, -1, 0, 1)
        ]
        flux = interface_flux(cells, 1)
        for f in range(5):
            line_x[t, pl.ds(f, 8, stride=8), :] = flux[f]
    for copy in edge_copies:
        copy.wait_recv()
    cols_x[0:8] = edge_recv[1]
    cols_x[520:528] = edge_recv[0]
    for f5 in range(2):
        cells = [
            [
                shift_lanes(cols_x[pl.ds(8 + k + 512 * f5, 8, stride=64), :], -(22 * f + 3))
                for f in range(5)
            ]
            for k in (-2, -1, 0, 1)
        ]
        flux = interface_flux(cells, 2)
        for f in range(5):
            line_y[pl.ds(64 * f5 + f, 8, stride=8), :] = flux[f]
    scale_y = jnp.where(lane < 4, HALF_STEP, -HALF_STEP)
    for r in range(4):
        for t in range(4):
            low = line_x[t, 8 * r : 8 * r + 8]
            high = line_x[t, 8 * r + 8 : 8 * r + 16]
            own_x[8 * r + 2 * t] = scale_x * jnp.where(first_lane, low, shift_lanes(high, 64))
            own_x[8 * r + 2 * t + 1] = scale_x * jnp.where(first_lane, shift_lanes(low, 64), high)
        for c in range(8):
            low = line_y[8 * c : 8 * c + 8]
            high = line_y[8 * c + 8 : 8 * c + 16]
            own_y[8 * r + c] = scale_y * jnp.where(
                lane < 4, shift_lanes(low, -4 * r), shift_lanes(high, 4 - 4 * r)
            )

    def wait_boxes(o, carry):
        box_copy(o).wait_recv()
        return carry

    def wait_ghosts(o, carry):
        ghost_copy(o).wait_recv()
        return carry

    lax.fori_loop(1, GROUP, wait_boxes, 0)
    lax.fori_loop(1, GROUP, wait_ghosts, 0)
    side_parts = [jnp.zeros((8, 128), F32) for _ in range(5)]
    for b in range(8):
        at = 8 * me + b
        device = tabs[T_DEV, at] & 15
        local = tabs[T_LOC, at] & 7
        owner = tabs[T_OWN, at] & 15
        second = tabs[T_RANK, at] == 1
        stays = device == me
        for f in range(5):
            box = jnp.where(stays, boxes[local, f], box_recv[device, f])
            inner = ghost_recv[owner, f]
            inner = jnp.where(second, shift_lanes(inner, 64), inner)
            mixed[f, 16 * b : 16 * b + 8] = inner
            mixed[f, 16 * b + 8 : 16 * b + 16] = box
        column = tabs[T_SPOT, at] & 7
        low_edge = ghost_recv[(owner + 15) & 15, 6]
        high_edge = ghost_recv[(owner + 1) & 15, 6]
        side = ghost_recv[owner, 5]
        side = jnp.where((sub < 3) & (column == 0), low_edge, side)
        side = jnp.where((sub >= 5) & (column == 7), high_edge, side)
        side = jnp.where(second, shift_lanes(side, -50), side)
        for f in range(5):
            side_parts[f] = jnp.where((lane >> 4) == b, shift_lanes(side, 16 * b - 10 * f), side_parts[f])

    ring = (lane - 4) & 127
    row = ring & 15
    base = ring - row
    coarse_row = (row >> 1) + 1

    def kept(i):
        return jnp.where(i < 4, i, jnp.where(i < 6, 3, i - 2))

    inner_index = [base + kept(coarse_row + d) for d in (0, -1, 1)]
    side_rows = [base + coarse_row + d for d in (0, -1, 1)]
    interior = (lane & 8) != 0
    row_sign = jnp.where((row & 1) == 0, -0.25, 0.25)
    for f in range(5):
        turned[f] = mixed[f].T
        for k in range(8):
            block = turned[f, 8 * k : 8 * k + 8]
            mid, low, high = [pick_lanes(block, index) for index in inner_index]
            coarse_c[f, 3 + 8 * k : 11 + 8 * k] = mid
            coarse_s[f, 3 + 8 * k : 11 + 8 * k] = row_sign * minmod(mid - low, high - mid)
        mid, low, high = [pick_lanes(side_parts[f], index) for index in side_rows]
        slope = row_sign * minmod(mid - low, high - mid)
        coarse_c[f, 0:4] = mid[0:4]
        coarse_c[f, 66:70] = mid[4:8]
        coarse_s[f, 0:4] = slope[0:4]
        coarse_s[f, 66:70] = slope[4:8]
        for k in range(9):
            j = 1 + 8 * k
            mid = coarse_c[f, j : j + 8]
            slope = minmod(mid - coarse_c[f, j - 1 : j + 7], coarse_c[f, j + 1 : j + 9] - mid)
            middle = mid + coarse_s[f, j : j + 8]
            state_a[f, pl.ds(2 * j - 2, 8, stride=2), :] = middle - 0.25 * slope
            state_a[f, pl.ds(2 * j - 1, 8, stride=2), :] = middle + 0.25 * slope
        for k in range(16):
            m = 4 + 8 * k
            state_a[f, m : m + 8] = jnp.where(interior, turned[f, 8 * k : 8 * k + 8], state_a[f, m : m + 8])

    lower_face = (lane & 15) == 7

    def y_sides(state, m):
        lower, upper = cell_sides(
            [state[f, m : m + 8] for f in range(5)],
            [state[f, m + 1 : m + 9] for f in range(5)],
            [state[f, m + 2 : m + 10] for f in range(5)],
            2,
        )
        for f in range(5):
            low_y[f, m + 9 : m + 17] = lower[f]
            high_y[f, m + 9 : m + 17] = upper[f]

    def y_change(f, m):
        after = high_y[f, m + 8 : m + 16] + low_y[f, m + 9 : m + 17]
        before = high_y[f, m + 7 : m + 15] + low_y[f, m + 8 : m + 16]
        return after - before

    def x_sides(state, m):
        cells = [state[f, m : m + 8] for f in range(5)]
        lower, upper = cell_sides(
            [shift_lanes(u, 1) for u in cells], cells, [shift_lanes(u, -1) for u in cells], 1
        )
        for f in range(5):
            low_x[f, m : m + 8] = lower[f]
            high_x[f, m : m + 8] = upper[f]

    def x_fluxes(f, m):
        lower = low_x[f, m : m + 8]
        upper = high_x[f, m : m + 8]
        return upper + shift_lanes(lower, -1), shift_lanes(upper, 1) + lower

    def y_faces(add):
        for f in range(5):
            for i, m in enumerate((3, 131)):
                flux = high_y[f, m + 8 : m + 9] + low_y[f, m + 9 : m + 10]
                faces_y[i, f : f + 1] = faces_y[i, f : f + 1] + flux if add else flux

    def first_step(m):
        for f in range(5):
            after, before = x_fluxes(f, m)
            faces_x[f, m : m + 8] = jnp.where(lower_face, after, before)
            state_b[f, m : m + 8] = state_a[f, m : m + 8] - HALF_STEP * ((after - before) + y_change(f, m))

    for m in range(0, 136, 8):
        y_sides(state_a, m)
        x_sides(state_a, m)
    for m in range(0, 136, 8):
        first_step(m)
    y_faces(False)

    def second_step_x(m):
        for f in range(5):
            after, before = x_fluxes(f, m)
            faces_x[f, m : m + 8] = faces_x[f, m : m + 8] + jnp.where(lower_face, after, before)
            change_x[f, m : m + 8] = after - before

    for m in range(0, 136, 8):
        x_sides(state_b, m)
    for m in range(0, 136, 8):
        second_step_x(m)
    y_sides(state_b, 0)
    y_sides(state_b, 128)
    y_faces(True)
    box_lane = 16 * (lane & 7)
    face_index = jnp.where((lane & 8) == 0, box_lane + 7, (box_lane + 16) & 127)
    for k in range(8):
        m = 4 + 16 * k
        block = jnp.zeros((8, 128), F32)
        for f in range(5):
            pairs = faces_x[f, pl.ds(m, 8, stride=2), :] + faces_x[f, pl.ds(m + 1, 8, stride=2), :]
            block = jnp.where((lane >> 4) == f, pick_lanes(pairs, face_index), block)
        face_cols[8 * k : 8 * k + 8] = block
    face_rows[...] = face_cols[...].T
    for f in range(5):
        low = face_rows[16 * f : 16 * f + 8]
        high = face_rows[16 * f + 8 : 16 * f + 16]
        sums_x[pl.ds(f, 8, stride=8), :] = jnp.where(first_lane, low, shift_lanes(high, 64))
    low = faces_y[0] + shift_lanes(faces_y[0], -1)
    high = faces_y[1] + shift_lanes(faces_y[1], -1)
    for b in range(8):
        index = 16 * b + 8 + 2 * (lane & 3)
        sums_y[b] = jnp.where((lane & 4) == 0, pick_lanes(low, index), pick_lanes(high, index))

    def pack_sums(o, dest, slot):
        at = 8 * peer(o)
        first = tabs[T_BACK, at] & 7
        second = tabs[T_BACK + 1, at] & 7
        dest[slot, 0:8] = sums_x[pl.ds(8 * first, 8), :]
        dest[slot, 5:13] = sums_x[pl.ds(8 * second, 8), :]
        dest[slot, 10:16] = jnp.where(lane < 8, sums_y[first], sums_y[second])[0:6]

    def send_sums(o, carry):
        pack_sums(o, sum_send, o)
        sum_copy(o).start()
        return carry

    def wait_sums(o, carry):
        sum_copy(o).wait_recv()
        return carry

    lax.fori_loop(1, GROUP, send_sums, 0)
    pack_sums(0, sum_recv, me)

    for m in range(8, 128, 8):
        y_sides(state_b, m)
    for m in range(0, 136, 8):
        for f in range(5):
            state_a[f, m : m + 8] = state_b[f, m : m + 8] - HALF_STEP * (change_x[f, m : m + 8] + y_change(f, m))
    for f in range(5):
        back[f] = state_a[f, 4:132].T
        for b in range(8):
            fine_out[b, f] = back[f, 16 * b + 8 : 16 * b + 16]

    for copy in halo_copies + edge_copies:
        copy.wait_send()

    def wait_sent(o, carry):
        box_copy(o).wait_send()
        ghost_copy(o).wait_send()
        return carry

    lax.fori_loop(1, GROUP, wait_sent, 0)
    lax.fori_loop(1, GROUP, wait_sums, 0)

    sign_x = jnp.where(first_lane, SUM_SCALE, -SUM_SCALE)
    for n in range(32):
        entry = tabs[T_INV, n]
        live = entry > 0
        slot = (entry - 1) & 31
        sender = slot >> 1
        second = (slot & 1) == 1
        total_x = sum_recv[sender, pl.ds(5 * (slot & 1), 8), :]
        total_y = sum_recv[sender, pl.ds(10, 6), :]
        total_y = jnp.where(second, pltpu.roll(total_y, 120, axis=1), total_y)
        sign_y = jnp.where(lane[0:5] < 4, SUM_SCALE, -SUM_SCALE)
        out_x[pl.ds(n, 5, stride=32), :] = jnp.where(live, own_x[n, 0:5] - sign_x[0:5] * total_x[0:5], 0.0)
        out_y[pl.ds(n, 5, stride=32), :] = jnp.where(live, own_y[n, 0:5] - sign_y * total_y[0:5], 0.0)
    for f in range(5):
        reflux_out[f, :, 0:128] = out_x[32 * f : 32 * f + 32]
        reflux_out[f, :, 128:136] = out_y[32 * f : 32 * f + 32][:, 0:8]

    def wait_sums_sent(o, carry):
        sum_copy(o).wait_send()
        return carry

    lax.fori_loop(1, GROUP, wait_sums_sent, 0)


def write_out(fine_in, reflux_in, fine_out, reflux_out, sems):
    copies = [
        pltpu.make_async_copy(fine_in, fine_out, sems.at[0]),
        pltpu.make_async_copy(reflux_in, reflux_out, sems.at[1]),
    ]
    for copy in copies:
        copy.start()
    for copy in copies:
        copy.wait()


def local(previous_fine_boxes, coarse_state, new_source, box_position):
    vmem = pl.BlockSpec(memory_space=pltpu.VMEM)
    hbm = pl.BlockSpec(memory_space=pltpu.HBM)
    dma = pltpu.SemaphoreType.DMA
    v = pltpu.VMEM
    fine, reflux = pl.pallas_call(
        body,
        out_shape=(
            jax.ShapeDtypeStruct((8, 5, 8, 128), F32),
            jax.ShapeDtypeStruct((5, 32, 136), F32),
        ),
        in_specs=[hbm] * 4,
        out_specs=(vmem, vmem),
        scratch_shapes=[
            v((8, 5, 8, 128), F32),
            v((5, 16, 512), F32),
            v((8, 128), I32),
            v((8, 128), I32),
            v((16, 128), I32),
            pltpu.SMEM((16, 128), I32),
            v((40, 48, 128), F32),
            v((4, 128, 128), F32),
            v((1040, 128), F32),
            v((2, 4, 16, 128), F32),
            v((2, 4, 16, 128), F32),
            v((2, 8, 128), F32),
            v((16, 5, 8, 128), F32),
            v((16, 5, 8, 128), F32),
            v((16, 7, 8, 128), F32),
            v((16, 7, 8, 128), F32),
            v((16, 16, 128), F32),
            v((16, 16, 128), F32),
            v((5, 128, 128), F32),
            v((5, 128, 128), F32),
            v((5, 80, 128), F32),
            v((5, 80, 128), F32),
            v((5, 152, 128), F32),
            v((5, 152, 128), F32),
            v((5, 160, 128), F32),
            v((5, 160, 128), F32),
            v((5, 136, 128), F32),
            v((5, 136, 128), F32),
            v((5, 136, 128), F32),
            v((5, 152, 128), F32),
            v((2, 8, 128), F32),
            v((128, 128), F32),
            v((128, 128), F32),
            v((5, 128, 128), F32),
            v((72, 128), F32),
            v((8, 8, 128), F32),
            v((4, 72, 128), F32),
            v((136, 128), F32),
            v((32, 8, 128), F32),
            v((32, 8, 128), F32),
            v((192, 128), F32),
            v((192, 128), F32),
            dma,
            dma((4,)),
            dma((4,)),
            dma((4,)),
            dma((16,)),
            dma((16,)),
            dma((16,)),
            dma((16,)),
            dma((16,)),
            dma((16,)),
        ],
        compiler_params=pltpu.CompilerParams(
            collective_id=0, has_side_effects=True, vmem_limit_bytes=64000 * 1024
        ),
    )(
        previous_fine_boxes,
        coarse_state,
        new_source.reshape(8, 128),
        box_position.reshape(8, 128),
    )
    fine, reflux = pl.pallas_call(
        write_out,
        out_shape=(
            jax.ShapeDtypeStruct((8, 5, 8, 128), F32),
            jax.ShapeDtypeStruct((5, 32, 136), F32),
        ),
        in_specs=[vmem] * 2,
        out_specs=(hbm, hbm),
        scratch_shapes=[dma((2,))],
    )(fine, reflux)
    return fine, jnp.transpose(reflux, (1, 0, 2))


def solution(mesh):
    placed = (P(("gx", "gy"), None, None, None), P(None, "gx", "gy"), P(), P())
    return jax.shard_map(
        local,
        mesh=mesh,
        in_specs=placed,
        out_specs=(P(("gx", "gy"), None, None, None), P(("gx", "gy"), None, None)),
        check_vma=False,
    )
```

```python
import jax
import jax.numpy as jnp
from jax import lax
from jax.experimental import pallas as pl
from jax.experimental.pallas import tpu as pltpu
from jax.sharding import PartitionSpec as P

MESH = pl.DeviceIdType.MESH
F32 = jnp.float32
I32 = jnp.int32

GROUP = 16
SLABS = 8
GAMMA_LESS = 0.4
STEP_RATIO = 0.15
WAVE_SPEED = 2.5
HALF_STEP = 0.5 * STEP_RATIO
SUM_SCALE = 0.25 * STEP_RATIO * 0.5

T_DEV, T_LOC, T_OWN, T_RANK, T_SPOT, T_BOX, T_INV = 0, 1, 2, 3, 4, 5, 6
T_POS, T_POS_NEXT, T_POS_BEFORE, T_BACK = 8, 10, 12, 14


def iota(axis):
    return lax.broadcasted_iota(I32, (8, 128), axis)


def shift_lanes(x, by):
    by = by % 128
    return x if by == 0 else pltpu.roll(x, by, axis=1)


def pick_lanes(x, index):
    return jnp.take_along_axis(x, index, axis=1)


def minmod(a, b):
    return jnp.maximum(jnp.minimum(a, b), jnp.minimum(jnp.maximum(a, b), 0.0))


def scaled_flux(state, along, sign):
    rho, m1, m2, m3, energy = state
    speed = sign * WAVE_SPEED
    inverse = 1.0 / rho
    pressure = GAMMA_LESS * (energy - 0.5 * (m1 * m1 + m2 * m2 + m3 * m3) * inverse)
    normal = state[along] * inverse
    moved = normal + speed
    pieces = [
        state[along] + speed * rho, m1 * moved, m2 * moved, m3 * moved, energy * moved + pressure * normal
    ]
    pieces[along] = pieces[along] + pressure
    return pieces


def cell_sides(low, mid, high, along):
    half = [0.5 * minmod(m - l, h - m) for l, m, h in zip(low, mid, high)]
    lower = scaled_flux([m - s for m, s in zip(mid, half)], along, -1.0)
    upper = scaled_flux([m + s for m, s in zip(mid, half)], along, 1.0)
    return lower, upper


def interface_flux(cells, along):
    a, b, c, d = cells
    left = [y + 0.5 * minmod(y - x, z - y) for x, y, z in zip(a, b, c)]
    right = [y - 0.5 * minmod(y - x, z - y) for x, y, z in zip(b, c, d)]
    upper = scaled_flux(left, along, 1.0)
    lower = scaled_flux(right, along, -1.0)
    return [u + l for u, l in zip(upper, lower)]


def make_tables(src_ref, pos_ref, gx, me, table):
    lane = iota(1)
    sub = iota(0)
    src = jnp.broadcast_to(src_ref[pl.ds(gx, 1), :], (8, 128)) & 127
    pos = jnp.broadcast_to(pos_ref[pl.ds(gx, 1), :], (8, 128)) & 511
    place = pick_lanes(pos, src)
    device = src >> 3
    local = src & 7
    owner = place >> 5
    spot = place & 31
    within = lane & 7
    group = lane >> 3
    rank = jnp.zeros((8, 128), I32)
    for d in range(1, 8):
        rank = rank + jnp.where((within >= d) & (shift_lanes(owner, d) == owner), 1, 0)

    def group_sum(v):
        for d in (1, 2, 4):
            v = v + shift_lanes(v, -d)
        return v

    mine = 8 * me + within
    my_owner = pick_lanes(owner, mine)
    my_rank = pick_lanes(rank, mine)
    after = (me + 1) & 15
    before = (me + 15) & 15
    rows = [device, local, owner, rank, spot, group_sum(jnp.where(device == me, local, 0)) & 7]
    inverse = jnp.zeros((8, 128), I32)
    for block in range(4):
        number = sub + 8 * block
        v = jnp.where((owner == me) & (spot == number), group * 2 + rank + 1, 0)
        for d in (64, 32, 16, 8, 4, 2, 1):
            v = v + shift_lanes(v, d)
        inverse = inverse + jnp.where(lane == number, v, 0)
    for d in (4, 2, 1):
        inverse = inverse + pltpu.roll(inverse, d, axis=0)
    rows += [jnp.minimum(inverse, 32), rank]
    for whose in (me, after, before):
        for a in range(2):
            rows.append(group_sum(jnp.where((owner == whose) & (rank == a), spot, 0)) & 31)
    for a in range(2):
        rows.append(group_sum(jnp.where((my_owner == group) & (my_rank == a), within, 0)) & 7)
    for i, row in enumerate(rows):
        table[pl.ds(i, 1), :] = row[0:1, :]


def body(
    boxes_in, coarse_in, maps_in, fine_out, reflux_out,
    boxes, coarse, src_ref, pos_ref, table, tabs, rim, rows_x, cols_x, halo_send, halo_recv, edge_recv,
    box_send, box_recv, ghost_send, ghost_recv, sum_send, sum_recv,
    mixed, turned, coarse_c, coarse_s, state_a, state_b, low_y, high_y, low_x, high_x, change_x, faces_x, faces_y,
    face_cols, face_rows, back, sums_x, sums_y, line_x, line_y, own_x, own_y, out_x, out_y,
    table_sem, in_sem, halo_ss, halo_rs, box_ss, box_rs, ghost_ss, ghost_rs, sum_ss, sum_rs,
):
    gx = lax.axis_index("gx")
    me = lax.axis_index("gy")
    lane = iota(1)
    sub = iota(0)

    def peer(o):
        return lax.rem(me + o, GROUP)

    def slab(o):
        return lax.rem(gx + o + SLABS, SLABS)

    near = [(slab(1), me), (slab(-1), me)]
    beside = [(gx, peer(GROUP - 1)), (gx, peer(1))]
    barrier = pltpu.get_barrier_semaphore()
    for there in near:
        pl.semaphore_signal(barrier, inc=1, device_id=there, device_id_type=MESH)
    for o in (1, 15, 4, 12, 2, 14, 8, 3, 13, 5, 11, 6, 10, 7, 9):
        pl.semaphore_signal(barrier, inc=1, device_id=(gx, peer(o)), device_id_type=MESH)
    fetches = [
        pltpu.make_async_copy(coarse_in, coarse, in_sem.at[0]),
        pltpu.make_async_copy(maps_in.at[0], src_ref, in_sem.at[1]),
        pltpu.make_async_copy(maps_in.at[1], pos_ref, in_sem.at[2]),
        pltpu.make_async_copy(boxes_in, boxes, in_sem.at[3]),
    ]
    for fetch in fetches:
        fetch.start()

    fetches[1].wait()
    fetches[2].wait()
    make_tables(src_ref, pos_ref, gx, me, table)
    to_scalars = pltpu.make_async_copy(table, tabs, table_sem)
    to_scalars.start()

    fetches[0].wait()
    for t in range(4):
        for f in range(5):
            tile = coarse[f, :, t * 128 : t * 128 + 128]
            halo_send[0, t, 3 * f : 3 * f + 3] = tile[13:16]
            halo_send[1, t, 3 * f : 3 * f + 3] = tile[0:3]
            rim[t * 5 + f, 8:24] = tile
            rim[20 + t * 5 + f, 8:24] = pltpu.roll(tile, 64, axis=1)
            rows_x[t, 22 * f + 3 : 22 * f + 19] = tile

    pl.semaphore_wait(barrier, GROUP + 1)
    halo_copies = []
    for i, there in enumerate(near):
        halo_copies.append(
            pltpu.make_async_remote_copy(
                halo_send.at[i], halo_recv.at[i], halo_ss.at[i], halo_rs.at[i], there, MESH
            )
        )
    for copy in halo_copies:
        copy.start()

    to_scalars.wait()
    fetches[3].wait()

    def box_copy(o):
        return pltpu.make_async_remote_copy(
            box_send.at[o, pl.ds(0, 50)], box_recv.at[me, pl.ds(0, 50)], box_ss.at[o], box_rs.at[o], (gx, peer(o)), MESH
        )

    def ghost_copy(o):
        return pltpu.make_async_remote_copy(
            ghost_send.at[o, pl.ds(0, 44)], ghost_recv.at[me, pl.ds(0, 44)], ghost_ss.at[o], ghost_rs.at[o], (gx, peer(o)), MESH
        )

    def sum_copy(o):
        return pltpu.make_async_remote_copy(
            sum_send.at[o, pl.ds(0, 15)], sum_recv.at[me, pl.ds(0, 15)], sum_ss.at[o], sum_rs.at[o], (gx, peer(o)), MESH
        )

    first_lane = lane < 64

    def patches(at):
        spots = [tabs[T_POS, at] & 31, tabs[T_POS + 1, at] & 31]
        rs = [s >> 3 for s in spots]
        cs = [s & 7 for s in spots]
        ids = [(((c & 1) ^ a) * 4 + (c >> 1)) * 5 for a, c in enumerate(cs)]
        return rs, cs, ids

    def pack_own(at, dest, slot):
        rs, _, ids = patches(at)
        for f in range(5):
            parts = [
                jnp.where(
                    sub == 0, rim[ids[a] + f, pl.ds(4 * rs[a] + 8, 8), :], rim[ids[a] + f, pl.ds(4 * rs[a] + 10, 8), :]
                )
                for a in range(2)
            ]
            dest[slot, 40 + 2 * f : 42 + 2 * f] = jnp.where(first_lane, parts[0], parts[1])[0:2]

    def send_box(o, carry):
        at = 8 * peer(o)
        which = tabs[T_BOX, at] & 7
        for f in range(5):
            box_send[o, 8 * f : 8 * f + 8] = boxes[which, f]
        pack_own(at, box_send, o)
        box_copy(o).start()
        return carry

    lax.fori_loop(1, GROUP, send_box, 0)
    pack_own(8 * me, box_recv, me)

    for copy in halo_copies:
        copy.wait_recv()
    for t in range(4):
        for f in range(5):
            top = halo_recv[0, t, 3 * f : 3 * f + 3]
            bottom = halo_recv[1, t, 3 * f : 3 * f + 3]
            rim[t * 5 + f, 5:8] = top
            rim[t * 5 + f, 24:27] = bottom
            rim[20 + t * 5 + f, 5:8] = pltpu.roll(top, 64, axis=1)
            rim[20 + t * 5 + f, 24:27] = pltpu.roll(bottom, 64, axis=1)
            rows_x[t, 22 * f : 22 * f + 3] = top
            rows_x[t, 22 * f + 19 : 22 * f + 22] = bottom
    for t in range(4):
        cols_x[8 + 128 * t : 136 + 128 * t] = rows_x[t].T
    edge_copies = [
        pltpu.make_async_remote_copy(
            cols_x.at[pl.ds(at, 8)], edge_recv.at[i], halo_ss.at[2 + i], halo_rs.at[2 + i], there, MESH
        )
        for i, (at, there) in enumerate(zip((8, 512), beside))
    ]
    for copy in edge_copies:
        copy.start()

    top_rows = sub < 4
    tenth = jnp.zeros((8, 128), I32)
    for i in range(1, 12):
        tenth = tenth + jnp.where(lane >= 10 * i, 1, 0)
    side_index = jnp.where(lane < 100, 22 * jnp.where(tenth >= 5, tenth - 5, tenth) + lane - 10 * tenth, 0)

    def pack_ghosts(o, dest, slot):
        at = 8 * peer(o)
        rs, cs, ids = patches(at)
        for f in range(5):
            parts = [
                jnp.where(
                    sub < 3, rim[ids[a] + f, pl.ds(4 * rs[a] + 5, 8), :], rim[ids[a] + f, pl.ds(4 * rs[a] + 9, 8), :]
                )
                for a in range(2)
            ]
            dest[slot, 6 * f : 6 * f + 6] = jnp.where(first_lane, parts[0], parts[1])[0:6]
        sides = []
        for a in range(2):
            strip = jnp.where(
                top_rows, cols_x[pl.ds(64 * cs[a] + 5, 8), :], cols_x[pl.ds(64 * cs[a] + 67, 8), :]
            )
            sides.append(pick_lanes(strip, side_index + 4 * rs[a]))
        dest[slot, 30:38] = jnp.where(lane < 50, sides[0], sides[1])
        edge = jnp.where(sub < 3, cols_x[517:525], cols_x[5:13])
        edges = []
        for a in range(2):
            low = (tabs[T_POS_NEXT + a, at] & 31) >> 3
            high = (tabs[T_POS_BEFORE + a, at] & 31) >> 3
            edges.append(pick_lanes(edge, side_index + 4 * jnp.where(sub < 3, low, high)))
        dest[slot, 38:44] = jnp.where(lane < 50, edges[0], edges[1])[0:6]

    def send_ghosts(o, carry):
        pack_ghosts(o, ghost_send, o)
        ghost_copy(o).start()
        return carry

    lax.fori_loop(1, GROUP, send_ghosts, 0)
    pack_ghosts(0, ghost_recv, me)

    scale_x = jnp.where(first_lane, HALF_STEP, -HALF_STEP)
    for t in range(4):
        cells = [
            [rim[t * 5 + f, pl.ds(8 + k, 8, stride=4), :] for f in range(5)] for k in (-2, -1, 0, 1)
        ]
        flux = interface_flux(cells, 1)
        for f in range(5):
            line_x[t, pl.ds(f, 8, stride=8), :] = flux[f]
    for copy in edge_copies:
        copy.wait_recv()
    cols_x[0:8] = edge_recv[1]
    cols_x[520:528] = edge_recv[0]
    for f5 in range(2):
        cells = [
            [
                shift_lanes(cols_x[pl.ds(8 + k + 512 * f5, 8, stride=64), :], -(22 * f + 3))
                for f in range(5)
            ]
            for k in (-2, -1, 0, 1)
        ]
        flux = interface_flux(cells, 2)
        for f in range(5):
            line_y[pl.ds(64 * f5 + f, 8, stride=8), :] = flux[f]
    scale_y = jnp.where(lane < 4, HALF_STEP, -HALF_STEP)
    for r in range(4):
        for t in range(4):
            low = line_x[t, 8 * r : 8 * r + 8]
            high = line_x[t, 8 * r + 8 : 8 * r + 16]
            own_x[8 * r + 2 * t] = scale_x * jnp.where(first_lane, low, shift_lanes(high, 64))
            own_x[8 * r + 2 * t + 1] = scale_x * jnp.where(first_lane, shift_lanes(low, 64), high)
        for c in range(8):
            low = line_y[8 * c : 8 * c + 8]
            high = line_y[8 * c + 8 : 8 * c + 16]
            own_y[8 * r + c] = scale_y * jnp.where(
                lane < 4, shift_lanes(low, -4 * r), shift_lanes(high, 4 - 4 * r)
            )

    def wait_boxes(o, carry):
        box_copy(o).wait_recv()
        return carry

    def wait_ghosts(o, carry):
        ghost_copy(o).wait_recv()
        return carry

    lax.fori_loop(1, GROUP, wait_boxes, 0)
    for b in range(8):
        at = 8 * me + b
        device = tabs[T_DEV, at] & 15
        local = tabs[T_LOC, at] & 7
        owner = tabs[T_OWN, at] & 15
        second = tabs[T_RANK, at] == 1
        stays = device == me
        for f in range(5):
            box = jnp.where(stays, boxes[local, f], box_recv[device, 8 * f : 8 * f + 8])
            mixed[f, 16 * b + 8 : 16 * b + 16] = box
            own = box_recv[owner, 40 + 2 * f : 42 + 2 * f]
            mixed[f, 16 * b + 6 : 16 * b + 8] = jnp.where(second, pltpu.roll(own, 64, axis=1), own)
    lax.fori_loop(1, GROUP, wait_ghosts, 0)
    side_parts = [jnp.zeros((8, 128), F32) for _ in range(5)]
    for b in range(8):
        at = 8 * me + b
        owner = tabs[T_OWN, at] & 15
        second = tabs[T_RANK, at] == 1
        for f in range(5):
            inner = ghost_recv[owner, 6 * f : 6 * f + 8]
            mixed[f, 16 * b : 16 * b + 6] = jnp.where(second, shift_lanes(inner, 64), inner)[0:6]
        column = tabs[T_SPOT, at] & 7
        low_edge = ghost_recv[(owner + 15) & 15, 38:46]
        high_edge = ghost_recv[(owner + 1) & 15, 36:44]
        side = ghost_recv[owner, 30:38]
        side = jnp.where((sub < 3) & (column == 0), low_edge, side)
        side = jnp.where((sub >= 5) & (column == 7), high_edge, side)
        side = jnp.where(second, shift_lanes(side, -50), side)
        for f in range(5):
            side_parts[f] = jnp.where((lane >> 4) == b, shift_lanes(side, 16 * b - 10 * f), side_parts[f])

    ring = (lane - 4) & 127
    row = ring & 15
    base = ring - row
    coarse_row = (row >> 1) + 1

    def kept(i):
        return jnp.where(i < 3, i, jnp.where(i < 6, 6, jnp.where(i == 6, 7, i - 4)))

    inner_index = [base + kept(coarse_row + d) for d in (0, -1, 1)]
    side_rows = [base + coarse_row + d for d in (0, -1, 1)]
    interior = (lane & 8) != 0
    row_sign = jnp.where((row & 1) == 0, -0.25, 0.25)
    for f in range(5):
        turned[f] = mixed[f].T
        for k in range(8):
            block = turned[f, 8 * k : 8 * k + 8]
            mid, low, high = [pick_lanes(block, index) for index in inner_index]
            coarse_c[f, 3 + 8 * k : 11 + 8 * k] = mid
            coarse_s[f, 3 + 8 * k : 11 + 8 * k] = row_sign * minmod(mid - low, high - mid)
        mid, low, high = [pick_lanes(side_parts[f], index) for index in side_rows]
        slope = row_sign * minmod(mid - low, high - mid)
        coarse_c[f, 0:4] = mid[0:4]
        coarse_c[f, 66:70] = mid[4:8]
        coarse_s[f, 0:4] = slope[0:4]
        coarse_s[f, 66:70] = slope[4:8]
        for k in range(9):
            j = 1 + 8 * k
            mid = coarse_c[f, j : j + 8]
            slope = minmod(mid - coarse_c[f, j - 1 : j + 7], coarse_c[f, j + 1 : j + 9] - mid)
            middle = mid + coarse_s[f, j : j + 8]
            state_a[f, pl.ds(2 * j - 2, 8, stride=2), :] = middle - 0.25 * slope
            state_a[f, pl.ds(2 * j - 1, 8, stride=2), :] = middle + 0.25 * slope
        for k in range(16):
            m = 4 + 8 * k
            state_a[f, m : m + 8] = jnp.where(interior, turned[f, 8 * k : 8 * k + 8], state_a[f, m : m + 8])

    lower_face = (lane & 15) == 7

    def y_sides(state, m):
        lower, upper = cell_sides(
            [state[f, m : m + 8] for f in range(5)],
            [state[f, m + 1 : m + 9] for f in range(5)],
            [state[f, m + 2 : m + 10] for f in range(5)],
            2,
        )
        for f in range(5):
            low_y[f, m + 9 : m + 17] = lower[f]
            high_y[f, m + 9 : m + 17] = upper[f]

    def y_change(f, m):
        after = high_y[f, m + 8 : m + 16] + low_y[f, m + 9 : m + 17]
        before = high_y[f, m + 7 : m + 15] + low_y[f, m + 8 : m + 16]
        return after - before

    def x_sides(state, m):
        cells = [state[f, m : m + 8] for f in range(5)]
        lower, upper = cell_sides(
            [shift_lanes(u, 1) for u in cells], cells, [shift_lanes(u, -1) for u in cells], 1
        )
        for f in range(5):
            low_x[f, m : m + 8] = lower[f]
            high_x[f, m : m + 8] = upper[f]

    def x_fluxes(f, m):
        lower = low_x[f, m : m + 8]
        upper = high_x[f, m : m + 8]
        return upper + shift_lanes(lower, -1), shift_lanes(upper, 1) + lower

    def y_faces(add):
        for f in range(5):
            for i, m in enumerate((3, 131)):
                flux = high_y[f, m + 8 : m + 9] + low_y[f, m + 9 : m + 10]
                faces_y[i, f : f + 1] = faces_y[i, f : f + 1] + flux if add else flux

    def first_step(m):
        for f in range(5):
            after, before = x_fluxes(f, m)
            faces_x[f, m : m + 8] = jnp.where(lower_face, after, before)
            state_b[f, m : m + 8] = state_a[f, m : m + 8] - HALF_STEP * ((after - before) + y_change(f, m))

    for m in range(0, 136, 8):
        y_sides(state_a, m)
        x_sides(state_a, m)
    for m in range(0, 136, 8):
        first_step(m)
    y_faces(False)

    def second_step_x(m):
        for f in range(5):
            after, before = x_fluxes(f, m)
            faces_x[f, m : m + 8] = faces_x[f, m : m + 8] + jnp.where(lower_face, after, before)
            change_x[f, m : m + 8] = after - before

    for m in range(0, 136, 8):
        x_sides(state_b, m)
    for m in range(0, 136, 8):
        second_step_x(m)
    y_sides(state_b, 0)
    y_sides(state_b, 128)
    y_faces(True)
    box_lane = 16 * (lane & 7)
    face_index = jnp.where((lane & 8) == 0, box_lane + 7, (box_lane + 16) & 127)
    for k in range(8):
        m = 4 + 16 * k
        block = jnp.zeros((8, 128), F32)
        for f in range(5):
            pairs = faces_x[f, pl.ds(m, 8, stride=2), :] + faces_x[f, pl.ds(m + 1, 8, stride=2), :]
            block = jnp.where((lane >> 4) == f, pick_lanes(pairs, face_index), block)
        face_cols[8 * k : 8 * k + 8] = block
    face_rows[...] = face_cols[...].T
    for f in range(5):
        low = face_rows[16 * f : 16 * f + 8]
        high = face_rows[16 * f + 8 : 16 * f + 16]
        sums_x[pl.ds(f, 8, stride=8), :] = jnp.where(first_lane, low, shift_lanes(high, 64))
    low = faces_y[0] + shift_lanes(faces_y[0], -1)
    high = faces_y[1] + shift_lanes(faces_y[1], -1)
    for b in range(8):
        index = 16 * b + 8 + 2 * (lane & 3)
        sums_y[b] = jnp.where((lane & 4) == 0, pick_lanes(low, index), pick_lanes(high, index))

    def pack_sums(o, dest, slot):
        at = 8 * peer(o)
        first = tabs[T_BACK, at] & 7
        second = tabs[T_BACK + 1, at] & 7
        dest[slot, 0:8] = sums_x[pl.ds(8 * first, 8), :]
        dest[slot, 5:13] = sums_x[pl.ds(8 * second, 8), :]
        dest[slot, 10:16] = jnp.where(lane < 8, sums_y[first], sums_y[second])[0:6]

    def send_sums(o, carry):
        pack_sums(o, sum_send, o)
        sum_copy(o).start()
        return carry

    def wait_sums(o, carry):
        sum_copy(o).wait_recv()
        return carry

    lax.fori_loop(1, GROUP, send_sums, 0)
    pack_sums(0, sum_recv, me)

    for m in range(8, 128, 8):
        y_sides(state_b, m)
    for m in range(0, 136, 8):
        for f in range(5):
            state_a[f, m : m + 8] = state_b[f, m : m + 8] - HALF_STEP * (change_x[f, m : m + 8] + y_change(f, m))
    for f in range(5):
        back[f] = state_a[f, 4:132].T
        for b in range(8):
            fine_out[b, f] = back[f, 16 * b + 8 : 16 * b + 16]

    for copy in halo_copies + edge_copies:
        copy.wait_send()

    def wait_sent(o, carry):
        box_copy(o).wait_send()
        ghost_copy(o).wait_send()
        return carry

    lax.fori_loop(1, GROUP, wait_sent, 0)
    lax.fori_loop(1, GROUP, wait_sums, 0)

    sign_x = jnp.where(first_lane, SUM_SCALE, -SUM_SCALE)
    for n in range(32):
        entry = tabs[T_INV, n]
        live = entry > 0
        slot = (entry - 1) & 31
        sender = slot >> 1
        second = (slot & 1) == 1
        total_x = sum_recv[sender, pl.ds(5 * (slot & 1), 8), :]
        total_y = sum_recv[sender, pl.ds(10, 6), :]
        total_y = jnp.where(second, pltpu.roll(total_y, 120, axis=1), total_y)
        sign_y = jnp.where(lane[0:5] < 4, SUM_SCALE, -SUM_SCALE)
        out_x[pl.ds(n, 5, stride=32), :] = jnp.where(live, own_x[n, 0:5] - sign_x[0:5] * total_x[0:5], 0.0)
        out_y[pl.ds(n, 5, stride=32), :] = jnp.where(live, own_y[n, 0:5] - sign_y * total_y[0:5], 0.0)
    for f in range(5):
        reflux_out[f, :, 0:128] = out_x[32 * f : 32 * f + 32]
        reflux_out[f, :, 128:136] = out_y[32 * f : 32 * f + 32][:, 0:8]

    def wait_sums_sent(o, carry):
        sum_copy(o).wait_send()
        return carry

    lax.fori_loop(1, GROUP, wait_sums_sent, 0)


def write_out(fine_in, reflux_in, fine_out, reflux_out, sems):
    copies = [
        pltpu.make_async_copy(fine_in, fine_out, sems.at[0]),
        pltpu.make_async_copy(reflux_in, reflux_out, sems.at[1]),
    ]
    for copy in copies:
        copy.start()
    for copy in copies:
        copy.wait()


def local(previous_fine_boxes, coarse_state, new_source, box_position):
    vmem = pl.BlockSpec(memory_space=pltpu.VMEM)
    hbm = pl.BlockSpec(memory_space=pltpu.HBM)
    dma = pltpu.SemaphoreType.DMA
    v = pltpu.VMEM
    fine, reflux = pl.pallas_call(
        body,
        out_shape=(
            jax.ShapeDtypeStruct((8, 5, 8, 128), F32),
            jax.ShapeDtypeStruct((5, 32, 136), F32),
        ),
        in_specs=[hbm] * 3,
        out_specs=(vmem, vmem),
        scratch_shapes=[
            v((8, 5, 8, 128), F32),
            v((5, 16, 512), F32),
            v((8, 128), I32),
            v((8, 128), I32),
            v((16, 128), I32),
            pltpu.SMEM((16, 128), I32),
            v((40, 48, 128), F32),
            v((4, 128, 128), F32),
            v((1040, 128), F32),
            v((2, 4, 16, 128), F32),
            v((2, 4, 16, 128), F32),
            v((2, 8, 128), F32),
            v((16, 56, 128), F32),
            v((16, 56, 128), F32),
            v((16, 48, 128), F32),
            v((16, 48, 128), F32),
            v((16, 16, 128), F32),
            v((16, 16, 128), F32),
            v((5, 128, 128), F32),
            v((5, 128, 128), F32),
            v((5, 80, 128), F32),
            v((5, 80, 128), F32),
            v((5, 152, 128), F32),
            v((5, 152, 128), F32),
            v((5, 160, 128), F32),
            v((5, 160, 128), F32),
            v((5, 136, 128), F32),
            v((5, 136, 128), F32),
            v((5, 136, 128), F32),
            v((5, 152, 128), F32),
            v((2, 8, 128), F32),
            v((128, 128), F32),
            v((128, 128), F32),
            v((5, 128, 128), F32),
            v((72, 128), F32),
            v((8, 8, 128), F32),
            v((4, 72, 128), F32),
            v((136, 128), F32),
            v((32, 8, 128), F32),
            v((32, 8, 128), F32),
            v((192, 128), F32),
            v((192, 128), F32),
            dma,
            dma((4,)),
            dma((4,)),
            dma((4,)),
            dma((16,)),
            dma((16,)),
            dma((16,)),
            dma((16,)),
            dma((16,)),
            dma((16,)),
        ],
        compiler_params=pltpu.CompilerParams(
            collective_id=0, has_side_effects=True, vmem_limit_bytes=54880 * 1024
        ),
    )(
        previous_fine_boxes,
        coarse_state,
        jnp.stack([new_source.reshape(8, 128), box_position.reshape(8, 128)]),
    )
    fine, reflux = pl.pallas_call(
        write_out,
        out_shape=(
            jax.ShapeDtypeStruct((8, 5, 8, 128), F32),
            jax.ShapeDtypeStruct((5, 32, 136), F32),
        ),
        in_specs=[vmem] * 2,
        out_specs=(hbm, hbm),
        scratch_shapes=[dma((2,))],
        compiler_params=pltpu.CompilerParams(vmem_limit_bytes=1024 * 1024),
    )(fine, reflux)
    return fine, jnp.transpose(reflux, (1, 0, 2))


def solution(mesh):
    placed = (P(("gx", "gy"), None, None, None), P(None, "gx", "gy"), P(), P())
    return jax.shard_map(
        local,
        mesh=mesh,
        in_specs=placed,
        out_specs=(P(("gx", "gy"), None, None, None), P(("gx", "gy"), None, None)),
        check_vma=False,
    )
```

```python
import jax
import jax.numpy as jnp
from jax import lax
from jax.experimental import pallas as pl
from jax.experimental.pallas import tpu as pltpu
from jax.sharding import PartitionSpec as P

MESH = pl.DeviceIdType.MESH
F32 = jnp.float32
I32 = jnp.int32

GROUP = 16
SLABS = 8
GAMMA_LESS = 0.4
STEP_RATIO = 0.15
WAVE_SPEED = 2.5
HALF_STEP = 0.5 * STEP_RATIO
SUM_SCALE = 0.25 * STEP_RATIO * 0.5

T_DEV, T_LOC, T_OWN, T_RANK, T_SPOT, T_BOX, T_INV = 0, 1, 2, 3, 4, 5, 6
T_POS, T_POS_NEXT, T_POS_BEFORE, T_BACK = 8, 10, 12, 14


def iota(axis):
    return lax.broadcasted_iota(I32, (8, 128), axis)


def shift_lanes(x, by):
    by = by % 128
    return x if by == 0 else pltpu.roll(x, by, axis=1)


def pick_lanes(x, index):
    return jnp.take_along_axis(x, index, axis=1)


def minmod(a, b):
    return jnp.maximum(jnp.minimum(a, b), jnp.minimum(jnp.maximum(a, b), 0.0))


def scaled_flux(state, along, sign):
    rho, m1, m2, m3, energy = state
    speed = sign * WAVE_SPEED
    inverse = 1.0 / rho
    pressure = GAMMA_LESS * (energy - 0.5 * (m1 * m1 + m2 * m2 + m3 * m3) * inverse)
    normal = state[along] * inverse
    moved = normal + speed
    pieces = [
        state[along] + speed * rho, m1 * moved, m2 * moved, m3 * moved, energy * moved + pressure * normal
    ]
    pieces[along] = pieces[along] + pressure
    return pieces


def cell_sides(low, mid, high, along):
    half = [0.5 * minmod(m - l, h - m) for l, m, h in zip(low, mid, high)]
    lower = scaled_flux([m - s for m, s in zip(mid, half)], along, -1.0)
    upper = scaled_flux([m + s for m, s in zip(mid, half)], along, 1.0)
    return lower, upper


def interface_flux(cells, along):
    a, b, c, d = cells
    left = [y + 0.5 * minmod(y - x, z - y) for x, y, z in zip(a, b, c)]
    right = [y - 0.5 * minmod(y - x, z - y) for x, y, z in zip(b, c, d)]
    upper = scaled_flux(left, along, 1.0)
    lower = scaled_flux(right, along, -1.0)
    return [u + l for u, l in zip(upper, lower)]


def make_tables(maps, gx, me, table):
    lane = iota(1)
    sub = iota(0)
    src = jnp.broadcast_to(maps[0, pl.ds(gx, 1), :], (8, 128)) & 127
    pos = jnp.broadcast_to(maps[1, pl.ds(gx, 1), :], (8, 128)) & 511
    place = pick_lanes(pos, src)
    device = src >> 3
    local = src & 7
    owner = place >> 5
    spot = place & 31
    within = lane & 7
    group = lane >> 3
    rank = jnp.zeros((8, 128), I32)
    for d in range(1, 8):
        rank = rank + jnp.where((within >= d) & (shift_lanes(owner, d) == owner), 1, 0)

    def group_sum(v):
        for d in (1, 2, 4):
            v = v + shift_lanes(v, -d)
        return v

    mine = 8 * me + within
    my_owner = pick_lanes(owner, mine)
    my_rank = pick_lanes(rank, mine)
    after = (me + 1) & 15
    before = (me + 15) & 15
    rows = [device, local, owner, rank, spot, group_sum(jnp.where(device == me, local, 0)) & 7]
    inverse = jnp.zeros((8, 128), I32)
    for block in range(4):
        number = sub + 8 * block
        v = jnp.where((owner == me) & (spot == number), group * 2 + rank + 1, 0)
        for d in (64, 32, 16, 8, 4, 2, 1):
            v = v + shift_lanes(v, d)
        inverse = inverse + jnp.where(lane == number, v, 0)
    for d in (4, 2, 1):
        inverse = inverse + pltpu.roll(inverse, d, axis=0)
    rows += [jnp.minimum(inverse, 32), rank]
    for whose in (me, after, before):
        for a in range(2):
            rows.append(group_sum(jnp.where((owner == whose) & (rank == a), spot, 0)) & 31)
    for a in range(2):
        rows.append(group_sum(jnp.where((my_owner == group) & (my_rank == a), within, 0)) & 7)
    for i, row in enumerate(rows):
        table[pl.ds(i, 1), :] = row[0:1, :]


def body(
    boxes_in, coarse_in, maps_in, fine_out, reflux_out,
    boxes, coarse, maps, table, tabs, rim, rows_x, cols_x, halo_send, halo_recv, edge_send, edge_recv,
    box_send, box_recv, ghost_send, ghost_recv, sum_send, sum_recv,
    mixed, turned, coarse_c, coarse_s, state_a, state_b, low_y, high_y, low_x, high_x, change_x, faces_x, faces_y,
    face_cols, face_rows, back, sums_x, sums_y, line_x, line_y, own_x, own_y, out_x, out_y,
    table_sem, coarse_sem, maps_sem, boxes_sem, halo_ss, halo_rs, edge_ss, edge_rs,
    box_ss, box_rs, ghost_ss, ghost_rs, sum_ss, sum_rs,
):
    gx = lax.axis_index("gx")
    me = lax.axis_index("gy")
    lane = iota(1)
    sub = iota(0)

    def peer(o):
        return lax.rem(me + o, GROUP)

    def slab(o):
        return lax.rem(gx + o + SLABS, SLABS)

    near = [(slab(1), me), (slab(-1), me)]
    beside = [(gx, peer(GROUP - 1)), (gx, peer(1))]
    barrier = pltpu.get_barrier_semaphore()
    for there in near:
        pl.semaphore_signal(barrier, inc=1, device_id=there, device_id_type=MESH)
    for o in (1, 15, 4, 12, 2, 14, 8, 3, 13, 5, 11, 6, 10, 7, 9):
        pl.semaphore_signal(barrier, inc=1, device_id=(gx, peer(o)), device_id_type=MESH)
    fetches = [
        pltpu.make_async_copy(coarse_in, coarse, coarse_sem),
        pltpu.make_async_copy(maps_in, maps, maps_sem),
        pltpu.make_async_copy(boxes_in, boxes, boxes_sem),
    ]
    for fetch in fetches:
        fetch.start()

    fetches[1].wait()
    make_tables(maps, gx, me, table)
    to_scalars = pltpu.make_async_copy(table, tabs, table_sem)
    to_scalars.start()

    fetches[0].wait()
    for t in range(4):
        for f in range(5):
            tile = coarse[f, :, t * 128 : t * 128 + 128]
            halo_send[0, t, 3 * f : 3 * f + 3] = tile[13:16]
            halo_send[1, t, 3 * f : 3 * f + 3] = tile[0:3]
            rim[t * 5 + f, 8:24] = tile
            rim[20 + t * 5 + f, 8:24] = pltpu.roll(tile, 64, axis=1)
            rows_x[t, 22 * f + 3 : 22 * f + 19] = tile

    pl.semaphore_wait(barrier, GROUP + 1)
    def halo_copy(part, there):
        return pltpu.make_async_remote_copy(
            halo_send.at[part], halo_recv.at[part], halo_ss, halo_rs, there, MESH
        )

    for i, there in enumerate(near):
        halo_copy(i, there).start()
    both_halos = halo_copy(pl.ds(0, 2), near[0])

    to_scalars.wait()
    fetches[2].wait()

    def group_copy(source, target, rows, sems, o):
        return pltpu.make_async_remote_copy(
            source.at[o, pl.ds(0, rows)], target.at[me, pl.ds(0, rows)], *sems, (gx, peer(o)), MESH
        )

    def whole_copy(source, target, rows, sems):
        parts = (pl.ds(0, GROUP - 1), pl.ds(0, rows))
        return pltpu.make_async_remote_copy(source.at[parts], target.at[parts], *sems, (gx, peer(1)), MESH)

    box_args = (box_send, box_recv, 50, (box_ss, box_rs))
    ghost_args = (ghost_send, ghost_recv, 44, (ghost_ss, ghost_rs))
    sum_args = (sum_send, sum_recv, 11, (sum_ss, sum_rs))

    first_lane = lane < 64

    def patches(at):
        spots = [tabs[T_POS, at] & 31, tabs[T_POS + 1, at] & 31]
        rs = [s >> 3 for s in spots]
        cs = [s & 7 for s in spots]
        ids = [(((c & 1) ^ a) * 4 + (c >> 1)) * 5 for a, c in enumerate(cs)]
        return rs, cs, ids

    def pack_own(at, dest, slot):
        rs, _, ids = patches(at)
        for f in range(5):
            parts = [
                jnp.where(
                    sub == 0, rim[ids[a] + f, pl.ds(4 * rs[a] + 8, 8), :], rim[ids[a] + f, pl.ds(4 * rs[a] + 10, 8), :]
                )
                for a in range(2)
            ]
            dest[slot, 40 + 2 * f : 42 + 2 * f] = jnp.where(first_lane, parts[0], parts[1])[0:2]

    def send_box(o, carry):
        at = 8 * peer(o)
        which = tabs[T_BOX, at] & 7
        for f in range(5):
            box_send[o, 8 * f : 8 * f + 8] = boxes[which, f]
        pack_own(at, box_send, o)
        group_copy(*box_args, o).start()
        return carry

    lax.fori_loop(1, GROUP, send_box, 0)
    pack_own(8 * me, box_recv, me)

    both_halos.wait_recv()
    for t in range(4):
        for f in range(5):
            top = halo_recv[0, t, 3 * f : 3 * f + 3]
            bottom = halo_recv[1, t, 3 * f : 3 * f + 3]
            rim[t * 5 + f, 5:8] = top
            rim[t * 5 + f, 24:27] = bottom
            rim[20 + t * 5 + f, 5:8] = pltpu.roll(top, 64, axis=1)
            rim[20 + t * 5 + f, 24:27] = pltpu.roll(bottom, 64, axis=1)
            rows_x[t, 22 * f : 22 * f + 3] = top
            rows_x[t, 22 * f + 19 : 22 * f + 22] = bottom
    for t in range(4):
        cols_x[8 + 128 * t : 136 + 128 * t] = rows_x[t].T
    def edge_copy(part, there):
        return pltpu.make_async_remote_copy(
            edge_send.at[part], edge_recv.at[part], edge_ss, edge_rs, there, MESH
        )

    for i, (at, there) in enumerate(zip((8, 512), beside)):
        edge_send[i] = cols_x[at : at + 8]
        edge_copy(i, there).start()
    both_edges = edge_copy(pl.ds(0, 2), beside[0])

    top_rows = sub < 4
    tenth = jnp.zeros((8, 128), I32)
    for i in range(1, 12):
        tenth = tenth + jnp.where(lane >= 10 * i, 1, 0)
    side_index = jnp.where(lane < 100, 22 * jnp.where(tenth >= 5, tenth - 5, tenth) + lane - 10 * tenth, 0)

    def pack_ghosts(o, dest, slot):
        at = 8 * peer(o)
        rs, cs, ids = patches(at)
        for f in range(5):
            parts = [
                jnp.where(
                    sub < 3, rim[ids[a] + f, pl.ds(4 * rs[a] + 5, 8), :], rim[ids[a] + f, pl.ds(4 * rs[a] + 9, 8), :]
                )
                for a in range(2)
            ]
            dest[slot, 6 * f : 6 * f + 6] = jnp.where(first_lane, parts[0], parts[1])[0:6]
        sides = []
        for a in range(2):
            strip = jnp.where(
                top_rows, cols_x[pl.ds(64 * cs[a] + 5, 8), :], cols_x[pl.ds(64 * cs[a] + 67, 8), :]
            )
            sides.append(pick_lanes(strip, side_index + 4 * rs[a]))
        dest[slot, 30:38] = jnp.where(lane < 50, sides[0], sides[1])
        edge = jnp.where(sub < 3, cols_x[517:525], cols_x[5:13])
        edges = []
        for a in range(2):
            low = (tabs[T_POS_NEXT + a, at] & 31) >> 3
            high = (tabs[T_POS_BEFORE + a, at] & 31) >> 3
            edges.append(pick_lanes(edge, side_index + 4 * jnp.where(sub < 3, low, high)))
        dest[slot, 38:44] = jnp.where(lane < 50, edges[0], edges[1])[0:6]

    def send_ghosts(o, carry):
        pack_ghosts(o, ghost_send, o)
        group_copy(*ghost_args, o).start()
        return carry

    lax.fori_loop(1, GROUP, send_ghosts, 0)
    pack_ghosts(0, ghost_recv, me)

    scale_x = jnp.where(first_lane, HALF_STEP, -HALF_STEP)
    for t in range(4):
        cells = [
            [rim[t * 5 + f, pl.ds(8 + k, 8, stride=4), :] for f in range(5)] for k in (-2, -1, 0, 1)
        ]
        flux = interface_flux(cells, 1)
        for f in range(5):
            line_x[t, pl.ds(f, 8, stride=8), :] = flux[f]
    both_edges.wait_recv()
    cols_x[0:8] = edge_recv[1]
    cols_x[520:528] = edge_recv[0]
    for f5 in range(2):
        cells = [
            [
                shift_lanes(cols_x[pl.ds(8 + k + 512 * f5, 8, stride=64), :], -(22 * f + 3))
                for f in range(5)
            ]
            for k in (-2, -1, 0, 1)
        ]
        flux = interface_flux(cells, 2)
        for f in range(5):
            line_y[pl.ds(64 * f5 + f, 8, stride=8), :] = flux[f]
    scale_y = jnp.where(lane < 4, HALF_STEP, -HALF_STEP)
    for r in range(4):
        for t in range(4):
            low = line_x[t, 8 * r : 8 * r + 8]
            high = line_x[t, 8 * r + 8 : 8 * r + 16]
            own_x[8 * r + 2 * t] = scale_x * jnp.where(first_lane, low, shift_lanes(high, 64))
            own_x[8 * r + 2 * t + 1] = scale_x * jnp.where(first_lane, shift_lanes(low, 64), high)
        for c in range(8):
            low = line_y[8 * c : 8 * c + 8]
            high = line_y[8 * c + 8 : 8 * c + 16]
            own_y[8 * r + c] = scale_y * jnp.where(
                lane < 4, shift_lanes(low, -4 * r), shift_lanes(high, 4 - 4 * r)
            )

    whole_copy(*box_args).wait_recv()
    for b in range(8):
        at = 8 * me + b
        device = tabs[T_DEV, at] & 15
        local = tabs[T_LOC, at] & 7
        owner = tabs[T_OWN, at] & 15
        second = tabs[T_RANK, at] == 1
        stays = device == me
        for f in range(5):
            box = jnp.where(stays, boxes[local, f], box_recv[device, 8 * f : 8 * f + 8])
            mixed[f, 16 * b + 8 : 16 * b + 16] = box
            own = box_recv[owner, 40 + 2 * f : 42 + 2 * f]
            mixed[f, 16 * b + 6 : 16 * b + 8] = jnp.where(second, pltpu.roll(own, 64, axis=1), own)
    whole_copy(*ghost_args).wait_recv()
    side_parts = [jnp.zeros((8, 128), F32) for _ in range(5)]
    for b in range(8):
        at = 8 * me + b
        owner = tabs[T_OWN, at] & 15
        second = tabs[T_RANK, at] == 1
        for f in range(5):
            inner = ghost_recv[owner, 6 * f : 6 * f + 8]
            mixed[f, 16 * b : 16 * b + 6] = jnp.where(second, shift_lanes(inner, 64), inner)[0:6]
        column = tabs[T_SPOT, at] & 7
        low_edge = ghost_recv[(owner + 15) & 15, 38:46]
        high_edge = ghost_recv[(owner + 1) & 15, 36:44]
        side = ghost_recv[owner, 30:38]
        side = jnp.where((sub < 3) & (column == 0), low_edge, side)
        side = jnp.where((sub >= 5) & (column == 7), high_edge, side)
        side = jnp.where(second, shift_lanes(side, -50), side)
        for f in range(5):
            side_parts[f] = jnp.where((lane >> 4) == b, shift_lanes(side, 16 * b - 10 * f), side_parts[f])

    ring = (lane - 4) & 127
    row = ring & 15
    base = ring - row
    coarse_row = (row >> 1) + 1

    def kept(i):
        return jnp.where(i < 3, i, jnp.where(i < 6, 6, jnp.where(i == 6, 7, i - 4)))

    inner_index = [base + kept(coarse_row + d) for d in (0, -1, 1)]
    side_rows = [base + coarse_row + d for d in (0, -1, 1)]
    interior = (lane & 8) != 0
    row_sign = jnp.where((row & 1) == 0, -0.25, 0.25)
    for f in range(5):
        turned[f] = mixed[f].T
        for k in range(8):
            block = turned[f, 8 * k : 8 * k + 8]
            mid, low, high = [pick_lanes(block, index) for index in inner_index]
            coarse_c[f, 3 + 8 * k : 11 + 8 * k] = mid
            coarse_s[f, 3 + 8 * k : 11 + 8 * k] = row_sign * minmod(mid - low, high - mid)
        mid, low, high = [pick_lanes(side_parts[f], index) for index in side_rows]
        slope = row_sign * minmod(mid - low, high - mid)
        coarse_c[f, 0:4] = mid[0:4]
        coarse_c[f, 66:70] = mid[4:8]
        coarse_s[f, 0:4] = slope[0:4]
        coarse_s[f, 66:70] = slope[4:8]
        for k in range(9):
            j = 1 + 8 * k
            mid = coarse_c[f, j : j + 8]
            slope = minmod(mid - coarse_c[f, j - 1 : j + 7], coarse_c[f, j + 1 : j + 9] - mid)
            middle = mid + coarse_s[f, j : j + 8]
            state_a[f, pl.ds(2 * j - 2, 8, stride=2), :] = middle - 0.25 * slope
            state_a[f, pl.ds(2 * j - 1, 8, stride=2), :] = middle + 0.25 * slope
        for k in range(16):
            m = 4 + 8 * k
            state_a[f, m : m + 8] = jnp.where(interior, turned[f, 8 * k : 8 * k + 8], state_a[f, m : m + 8])

    lower_face = (lane & 15) == 7

    def y_sides(state, m):
        lower, upper = cell_sides(
            [state[f, m : m + 8] for f in range(5)],
            [state[f, m + 1 : m + 9] for f in range(5)],
            [state[f, m + 2 : m + 10] for f in range(5)],
            2,
        )
        for f in range(5):
            low_y[f, m + 9 : m + 17] = lower[f]
            high_y[f, m + 9 : m + 17] = upper[f]

    def y_change(f, m):
        after = high_y[f, m + 8 : m + 16] + low_y[f, m + 9 : m + 17]
        before = high_y[f, m + 7 : m + 15] + low_y[f, m + 8 : m + 16]
        return after - before

    def x_sides(state, m):
        cells = [state[f, m : m + 8] for f in range(5)]
        lower, upper = cell_sides(
            [shift_lanes(u, 1) for u in cells], cells, [shift_lanes(u, -1) for u in cells], 1
        )
        for f in range(5):
            low_x[f, m : m + 8] = lower[f]
            high_x[f, m : m + 8] = upper[f]

    def x_fluxes(f, m):
        lower = low_x[f, m : m + 8]
        upper = high_x[f, m : m + 8]
        return upper + shift_lanes(lower, -1), shift_lanes(upper, 1) + lower

    def y_faces(add):
        for f in range(5):
            for i, m in enumerate((3, 131)):
                flux = high_y[f, m + 8 : m + 9] + low_y[f, m + 9 : m + 10]
                faces_y[i, f : f + 1] = faces_y[i, f : f + 1] + flux if add else flux

    def first_step(m):
        for f in range(5):
            after, before = x_fluxes(f, m)
            faces_x[f, m : m + 8] = jnp.where(lower_face, after, before)
            state_b[f, m : m + 8] = state_a[f, m : m + 8] - HALF_STEP * ((after - before) + y_change(f, m))

    for m in range(0, 136, 8):
        y_sides(state_a, m)
        x_sides(state_a, m)
    for m in range(0, 136, 8):
        first_step(m)
    y_faces(False)

    def second_step_x(m):
        for f in range(5):
            after, before = x_fluxes(f, m)
            faces_x[f, m : m + 8] = faces_x[f, m : m + 8] + jnp.where(lower_face, after, before)
            change_x[f, m : m + 8] = after - before

    for m in range(0, 136, 8):
        x_sides(state_b, m)
    for m in range(0, 136, 8):
        second_step_x(m)
    y_sides(state_b, 0)
    y_sides(state_b, 128)
    y_faces(True)
    box_lane = 16 * (lane & 7)
    face_index = jnp.where((lane & 8) == 0, box_lane + 7, (box_lane + 16) & 127)
    for k in range(8):
        m = 4 + 16 * k
        block = jnp.zeros((8, 128), F32)
        for f in range(5):
            pairs = faces_x[f, pl.ds(m, 8, stride=2), :] + faces_x[f, pl.ds(m + 1, 8, stride=2), :]
            block = jnp.where((lane >> 4) == f, pick_lanes(pairs, face_index), block)
        face_cols[8 * k : 8 * k + 8] = block
    face_rows[...] = face_cols[...].T
    for f in range(5):
        low = face_rows[16 * f : 16 * f + 8]
        high = face_rows[16 * f + 8 : 16 * f + 16]
        sums_x[pl.ds(f, 8, stride=8), :] = jnp.where(first_lane, low, shift_lanes(high, 64))
    low = faces_y[0] + shift_lanes(faces_y[0], -1)
    high = faces_y[1] + shift_lanes(faces_y[1], -1)
    field = jnp.where(lane < 40, lane >> 3, (lane >> 3) - 5)
    for b in range(8):
        index = 16 * b + 8 + 2 * (lane & 3)
        both = jnp.where((lane & 4) == 0, pick_lanes(low, index), pick_lanes(high, index))
        sums_y[b : b + 1] = jnp.sum(jnp.where(sub == field, both, 0.0), axis=0, keepdims=True)

    def pack_sums(o, dest, slot):
        at = 8 * peer(o)
        first = tabs[T_BACK, at] & 7
        second = tabs[T_BACK + 1, at] & 7
        dest[slot, 0:8] = sums_x[pl.ds(8 * first, 8), :]
        dest[slot, 5:13] = sums_x[pl.ds(8 * second, 8), :]
        dest[slot, 10:11] = jnp.where(lane[0:1] < 40, sums_y[pl.ds(first, 1)], sums_y[pl.ds(second, 1)])

    def send_sums(o, carry):
        pack_sums(o, sum_send, o)
        group_copy(*sum_args, o).start()
        return carry

    lax.fori_loop(1, GROUP, send_sums, 0)
    pack_sums(0, sum_recv, me)

    for m in range(8, 128, 8):
        y_sides(state_b, m)
    for m in range(0, 136, 8):
        for f in range(5):
            state_a[f, m : m + 8] = state_b[f, m : m + 8] - HALF_STEP * (change_x[f, m : m + 8] + y_change(f, m))
    for f in range(5):
        back[f] = state_a[f, 4:132].T
        for b in range(8):
            fine_out[b, f] = back[f, 16 * b + 8 : 16 * b + 16]

    both_halos.wait_send()
    both_edges.wait_send()
    whole_copy(*box_args).wait_send()
    whole_copy(*ghost_args).wait_send()
    whole_copy(*sum_args).wait_recv()

    sign_x = jnp.where(first_lane, SUM_SCALE, -SUM_SCALE)
    sign_y = jnp.where(lane < 4, SUM_SCALE, -SUM_SCALE)
    y_index = 8 * jnp.minimum(sub, 4) + (lane & 7)
    for n in range(32):
        entry = tabs[T_INV, n]
        live = entry > 0
        slot = (entry - 1) & 31
        sender = slot >> 1
        total_x = sum_recv[sender, pl.ds(5 * (slot & 1), 8), :]
        total_y = jnp.broadcast_to(sum_recv[sender, 10:11], (8, 128))
        total_y = pick_lanes(total_y, y_index + 40 * (slot & 1))
        out_x[pl.ds(n, 5, stride=32), :] = jnp.where(live, own_x[n, 0:5] - sign_x[0:5] * total_x[0:5], 0.0)
        out_y[pl.ds(n, 5, stride=32), :] = jnp.where(live, own_y[n, 0:5] - sign_y[0:5] * total_y[0:5], 0.0)
    for f in range(5):
        reflux_out[f, :, 0:128] = out_x[32 * f : 32 * f + 32]
        reflux_out[f, :, 128:136] = out_y[32 * f : 32 * f + 32][:, 0:8]

    whole_copy(*sum_args).wait_send()


def write_out(fine_in, reflux_in, fine_out, reflux_out, sems):
    copies = [
        pltpu.make_async_copy(fine_in, fine_out, sems.at[0]),
        pltpu.make_async_copy(reflux_in, reflux_out, sems.at[1]),
    ]
    for copy in copies:
        copy.start()
    for copy in copies:
        copy.wait()


def local(previous_fine_boxes, coarse_state, new_source, box_position):
    vmem = pl.BlockSpec(memory_space=pltpu.VMEM)
    hbm = pl.BlockSpec(memory_space=pltpu.HBM)
    dma = pltpu.SemaphoreType.DMA
    v = pltpu.VMEM
    fine, reflux = pl.pallas_call(
        body,
        out_shape=(
            jax.ShapeDtypeStruct((8, 5, 8, 128), F32),
            jax.ShapeDtypeStruct((5, 32, 136), F32),
        ),
        in_specs=[hbm] * 3,
        out_specs=(vmem, vmem),
        scratch_shapes=[
            v((8, 5, 8, 128), F32),
            v((5, 16, 512), F32),
            v((2, 8, 128), I32),
            v((16, 128), I32),
            pltpu.SMEM((16, 128), I32),
            v((40, 48, 128), F32),
            v((4, 128, 128), F32),
            v((1040, 128), F32),
            v((2, 4, 16, 128), F32),
            v((2, 4, 16, 128), F32),
            v((2, 8, 128), F32),
            v((2, 8, 128), F32),
            v((16, 56, 128), F32),
            v((16, 56, 128), F32),
            v((16, 48, 128), F32),
            v((16, 48, 128), F32),
            v((16, 16, 128), F32),
            v((16, 16, 128), F32),
            v((5, 128, 128), F32),
            v((5, 128, 128), F32),
            v((5, 80, 128), F32),
            v((5, 80, 128), F32),
            v((5, 152, 128), F32),
            v((5, 152, 128), F32),
            v((5, 160, 128), F32),
            v((5, 160, 128), F32),
            v((5, 136, 128), F32),
            v((5, 136, 128), F32),
            v((5, 136, 128), F32),
            v((5, 152, 128), F32),
            v((2, 8, 128), F32),
            v((128, 128), F32),
            v((128, 128), F32),
            v((5, 128, 128), F32),
            v((72, 128), F32),
            v((8, 128), F32),
            v((4, 72, 128), F32),
            v((136, 128), F32),
            v((32, 8, 128), F32),
            v((32, 8, 128), F32),
            v((192, 128), F32),
            v((192, 128), F32),
            *[dma] * 14,
        ],
        compiler_params=pltpu.CompilerParams(
            collective_id=0, has_side_effects=True, vmem_limit_bytes=54880 * 1024
        ),
    )(
        previous_fine_boxes,
        coarse_state,
        jnp.stack([new_source.reshape(8, 128), box_position.reshape(8, 128)]),
    )
    fine, reflux = pl.pallas_call(
        write_out,
        out_shape=(
            jax.ShapeDtypeStruct((8, 5, 8, 128), F32),
            jax.ShapeDtypeStruct((5, 32, 136), F32),
        ),
        in_specs=[vmem] * 2,
        out_specs=(hbm, hbm),
        scratch_shapes=[dma((2,))],
        compiler_params=pltpu.CompilerParams(vmem_limit_bytes=1024 * 1024),
    )(fine, reflux)
    return fine, jnp.transpose(reflux, (1, 0, 2))


def solution(mesh):
    placed = (P(("gx", "gy"), None, None, None), P(None, "gx", "gy"), P(), P())
    return jax.shard_map(
        local,
        mesh=mesh,
        in_specs=placed,
        out_specs=(P(("gx", "gy"), None, None, None), P(("gx", "gy"), None, None)),
        check_vma=False,
    )
```

```python
import jax
import jax.numpy as jnp
from jax import lax
from jax.experimental import pallas as pl
from jax.experimental.pallas import tpu as pltpu
from jax.sharding import PartitionSpec as P

MESH = pl.DeviceIdType.MESH
F32 = jnp.float32
I32 = jnp.int32

GROUP = 16
SLABS = 8
GAMMA_LESS = 0.4
STEP_RATIO = 0.15
WAVE_SPEED = 2.5
HALF_STEP = 0.5 * STEP_RATIO
SUM_SCALE = 0.25 * STEP_RATIO * 0.5

T_DEV, T_LOC, T_OWN, T_RANK, T_SPOT, T_BOX, T_INV = 0, 1, 2, 3, 4, 5, 6
T_POS, T_POS_NEXT, T_POS_BEFORE, T_BACK = 8, 10, 12, 14


def iota(axis):
    return lax.broadcasted_iota(I32, (8, 128), axis)


def shift_lanes(x, by):
    by = by % 128
    return x if by == 0 else pltpu.roll(x, by, axis=1)


def pick_lanes(x, index):
    return jnp.take_along_axis(x, index, axis=1)


def minmod(a, b):
    return jnp.maximum(jnp.minimum(a, b), jnp.minimum(jnp.maximum(a, b), 0.0))


def scaled_flux(state, along, sign):
    rho, m1, m2, m3, energy = state
    speed = sign * WAVE_SPEED
    inverse = 1.0 / rho
    pressure = GAMMA_LESS * (energy - 0.5 * (m1 * m1 + m2 * m2 + m3 * m3) * inverse)
    normal = state[along] * inverse
    moved = normal + speed
    pieces = [
        state[along] + speed * rho, m1 * moved, m2 * moved, m3 * moved, energy * moved + pressure * normal
    ]
    pieces[along] = pieces[along] + pressure
    return pieces


def cell_sides(low, mid, high, along):
    half = [0.5 * minmod(m - l, h - m) for l, m, h in zip(low, mid, high)]
    lower = scaled_flux([m - s for m, s in zip(mid, half)], along, -1.0)
    upper = scaled_flux([m + s for m, s in zip(mid, half)], along, 1.0)
    return lower, upper


def interface_flux(cells, along):
    a, b, c, d = cells
    left = [y + 0.5 * minmod(y - x, z - y) for x, y, z in zip(a, b, c)]
    right = [y - 0.5 * minmod(y - x, z - y) for x, y, z in zip(b, c, d)]
    upper = scaled_flux(left, along, 1.0)
    lower = scaled_flux(right, along, -1.0)
    return [u + l for u, l in zip(upper, lower)]


def make_tables(maps, gx, me, table):
    lane = iota(1)
    sub = iota(0)
    src = jnp.broadcast_to(maps[0, pl.ds(gx, 1), :], (8, 128)) & 127
    pos = jnp.broadcast_to(maps[1, pl.ds(gx, 1), :], (8, 128)) & 511
    place = pick_lanes(pos, src)
    device = src >> 3
    local = src & 7
    owner = place >> 5
    spot = place & 31
    within = lane & 7
    group = lane >> 3
    rank = jnp.zeros((8, 128), I32)
    for d in range(1, 8):
        rank = rank + jnp.where((within >= d) & (shift_lanes(owner, d) == owner), 1, 0)

    def group_sum(v):
        for d in (1, 2, 4):
            v = v + shift_lanes(v, -d)
        return v

    mine = 8 * me + within
    my_owner = pick_lanes(owner, mine)
    my_rank = pick_lanes(rank, mine)
    after = (me + 1) & 15
    before = (me + 15) & 15
    rows = [device, local, owner, rank, spot, group_sum(jnp.where(device == me, local, 0)) & 7]
    inverse = jnp.zeros((8, 128), I32)
    for block in range(4):
        number = sub + 8 * block
        v = jnp.where((owner == me) & (spot == number), group * 2 + rank + 1, 0)
        for d in (64, 32, 16, 8, 4, 2, 1):
            v = v + shift_lanes(v, d)
        inverse = inverse + jnp.where(lane == number, v, 0)
    for d in (4, 2, 1):
        inverse = inverse + pltpu.roll(inverse, d, axis=0)
    rows += [jnp.minimum(inverse, 32), rank]
    for whose in (me, after, before):
        for a in range(2):
            rows.append(group_sum(jnp.where((owner == whose) & (rank == a), spot, 0)) & 31)
    for a in range(2):
        rows.append(group_sum(jnp.where((my_owner == group) & (my_rank == a), within, 0)) & 7)
    for i, row in enumerate(rows):
        table[pl.ds(i, 1), :] = row[0:1, :]


def body(
    boxes_in, coarse_in, maps_in, fine_out, reflux_out,
    boxes, coarse, maps, table, tabs, rim, rows_x, cols_x, halo_send, halo_recv, edge_send, edge_recv,
    box_send, box_recv, ghost_send, ghost_recv, sum_send, sum_recv,
    mixed, turned, coarse_c, coarse_s, state_a, state_b, low_y, high_y, low_x, high_x, change_x, faces_x, faces_y,
    face_cols, face_rows, back, sums_x, sums_y, line_x, line_y, own_x, own_y, out_x, out_y,
    table_sem, coarse_sem, maps_sem, boxes_sem, halo_ss, halo_rs, edge_ss, edge_rs,
    box_ss, box_rs, ghost_ss, ghost_rs, sum_ss, sum_rs,
):
    gx = lax.axis_index("gx")
    me = lax.axis_index("gy")
    lane = iota(1)
    sub = iota(0)

    def peer(o):
        return lax.rem(me + o, GROUP)

    def slab(o):
        return lax.rem(gx + o + SLABS, SLABS)

    near = [(slab(1), me), (slab(-1), me)]
    beside = [(gx, peer(GROUP - 1)), (gx, peer(1))]
    barrier = pltpu.get_barrier_semaphore()
    for there in near:
        pl.semaphore_signal(barrier, inc=1, device_id=there, device_id_type=MESH)
    for o in (1, 15, 4, 12, 2, 14, 8, 3, 13, 5, 11, 6, 10, 7, 9):
        pl.semaphore_signal(barrier, inc=1, device_id=(gx, peer(o)), device_id_type=MESH)
    fetches = [
        pltpu.make_async_copy(coarse_in, coarse, coarse_sem),
        pltpu.make_async_copy(maps_in, maps, maps_sem),
        pltpu.make_async_copy(boxes_in, boxes, boxes_sem),
    ]
    for fetch in fetches:
        fetch.start()

    fetches[1].wait()
    make_tables(maps, gx, me, table)
    to_scalars = pltpu.make_async_copy(table, tabs, table_sem)
    to_scalars.start()

    fetches[0].wait()
    for t in range(4):
        for f in range(5):
            tile = coarse[f, :, t * 128 : t * 128 + 128]
            halo_send[0, t, 3 * f : 3 * f + 3] = tile[13:16]
            halo_send[1, t, 3 * f : 3 * f + 3] = tile[0:3]
            rim[t * 5 + f, 8:24] = tile
            rim[20 + t * 5 + f, 8:24] = pltpu.roll(tile, 64, axis=1)
            rows_x[t, 22 * f + 3 : 22 * f + 19] = tile

    to_scalars.wait()
    fetches[2].wait()

    first_lane = lane < 64

    def patches(at):
        spots = [tabs[T_POS, at] & 31, tabs[T_POS + 1, at] & 31]
        rs = [s >> 3 for s in spots]
        cs = [s & 7 for s in spots]
        ids = [(((c & 1) ^ a) * 4 + (c >> 1)) * 5 for a, c in enumerate(cs)]
        return rs, cs, ids

    def pack_own(at, dest, slot):
        rs, _, ids = patches(at)
        for f in range(5):
            parts = [
                jnp.where(
                    sub == 0, rim[ids[a] + f, pl.ds(4 * rs[a] + 8, 8), :], rim[ids[a] + f, pl.ds(4 * rs[a] + 10, 8), :]
                )
                for a in range(2)
            ]
            dest[slot, 40 + 2 * f : 42 + 2 * f] = jnp.where(first_lane, parts[0], parts[1])[0:2]

    def pack_box(o, carry):
        at = 8 * peer(o)
        which = tabs[T_BOX, at] & 7
        for f in range(5):
            box_send[o, 8 * f : 8 * f + 8] = boxes[which, f]
        pack_own(at, box_send, o)
        return carry

    lax.fori_loop(1, GROUP, pack_box, 0)
    pl.semaphore_wait(barrier, GROUP + 1)
    def halo_copy(part, there):
        return pltpu.make_async_remote_copy(
            halo_send.at[part], halo_recv.at[part], halo_ss, halo_rs, there, MESH
        )

    for i, there in enumerate(near):
        halo_copy(i, there).start()
    both_halos = halo_copy(pl.ds(0, 2), near[0])


    def group_copy(source, target, rows, sems, o):
        return pltpu.make_async_remote_copy(
            source.at[o, pl.ds(0, rows)], target.at[me, pl.ds(0, rows)], *sems, (gx, peer(o)), MESH
        )

    def whole_copy(source, target, rows, sems):
        parts = (pl.ds(0, GROUP - 1), pl.ds(0, rows))
        return pltpu.make_async_remote_copy(source.at[parts], target.at[parts], *sems, (gx, peer(1)), MESH)

    box_args = (box_send, box_recv, 50, (box_ss, box_rs))
    ghost_args = (ghost_send, ghost_recv, 44, (ghost_ss, ghost_rs))
    sum_args = (sum_send, sum_recv, 11, (sum_ss, sum_rs))

    def send_box(o, carry):
        group_copy(*box_args, o).start()
        return carry

    lax.fori_loop(1, GROUP, send_box, 0)
    pack_own(8 * me, box_recv, me)

    both_halos.wait_recv()
    for t in range(4):
        for f in range(5):
            top = halo_recv[0, t, 3 * f : 3 * f + 3]
            bottom = halo_recv[1, t, 3 * f : 3 * f + 3]
            rim[t * 5 + f, 5:8] = top
            rim[t * 5 + f, 24:27] = bottom
            rim[20 + t * 5 + f, 5:8] = pltpu.roll(top, 64, axis=1)
            rim[20 + t * 5 + f, 24:27] = pltpu.roll(bottom, 64, axis=1)
            rows_x[t, 22 * f : 22 * f + 3] = top
            rows_x[t, 22 * f + 19 : 22 * f + 22] = bottom
    for t in range(4):
        cols_x[8 + 128 * t : 136 + 128 * t] = rows_x[t].T
    def edge_copy(part, there):
        return pltpu.make_async_remote_copy(
            edge_send.at[part], edge_recv.at[part], edge_ss, edge_rs, there, MESH
        )

    for i, (at, there) in enumerate(zip((8, 512), beside)):
        edge_send[i] = cols_x[at : at + 8]
        edge_copy(i, there).start()
    both_edges = edge_copy(pl.ds(0, 2), beside[0])

    top_rows = sub < 4
    tenth = jnp.zeros((8, 128), I32)
    for i in range(1, 12):
        tenth = tenth + jnp.where(lane >= 10 * i, 1, 0)
    side_index = jnp.where(lane < 100, 22 * jnp.where(tenth >= 5, tenth - 5, tenth) + lane - 10 * tenth, 0)

    def pack_ghosts(o, dest, slot):
        at = 8 * peer(o)
        rs, cs, ids = patches(at)
        for f in range(5):
            parts = [
                jnp.where(
                    sub < 3, rim[ids[a] + f, pl.ds(4 * rs[a] + 5, 8), :], rim[ids[a] + f, pl.ds(4 * rs[a] + 9, 8), :]
                )
                for a in range(2)
            ]
            dest[slot, 6 * f : 6 * f + 6] = jnp.where(first_lane, parts[0], parts[1])[0:6]
        sides = []
        for a in range(2):
            strip = jnp.where(
                top_rows, cols_x[pl.ds(64 * cs[a] + 5, 8), :], cols_x[pl.ds(64 * cs[a] + 67, 8), :]
            )
            sides.append(pick_lanes(strip, side_index + 4 * rs[a]))
        dest[slot, 30:38] = jnp.where(lane < 50, sides[0], sides[1])
        edge = jnp.where(sub < 3, cols_x[517:525], cols_x[5:13])
        edges = []
        for a in range(2):
            low = (tabs[T_POS_NEXT + a, at] & 31) >> 3
            high = (tabs[T_POS_BEFORE + a, at] & 31) >> 3
            edges.append(pick_lanes(edge, side_index + 4 * jnp.where(sub < 3, low, high)))
        dest[slot, 38:44] = jnp.where(lane < 50, edges[0], edges[1])[0:6]

    def send_ghosts(o, carry):
        pack_ghosts(o, ghost_send, o)
        group_copy(*ghost_args, o).start()
        return carry

    lax.fori_loop(1, GROUP, send_ghosts, 0)
    pack_ghosts(0, ghost_recv, me)

    scale_x = jnp.where(first_lane, HALF_STEP, -HALF_STEP)
    for t in range(4):
        cells = [
            [rim[t * 5 + f, pl.ds(8 + k, 8, stride=4), :] for f in range(5)] for k in (-2, -1, 0, 1)
        ]
        flux = interface_flux(cells, 1)
        for f in range(5):
            line_x[t, pl.ds(f, 8, stride=8), :] = flux[f]
    both_edges.wait_recv()
    cols_x[0:8] = edge_recv[1]
    cols_x[520:528] = edge_recv[0]
    for f5 in range(2):
        cells = [
            [
                shift_lanes(cols_x[pl.ds(8 + k + 512 * f5, 8, stride=64), :], -(22 * f + 3))
                for f in range(5)
            ]
            for k in (-2, -1, 0, 1)
        ]
        flux = interface_flux(cells, 2)
        for f in range(5):
            line_y[pl.ds(64 * f5 + f, 8, stride=8), :] = flux[f]
    scale_y = jnp.where(lane < 4, HALF_STEP, -HALF_STEP)
    for r in range(4):
        for t in range(4):
            low = line_x[t, 8 * r : 8 * r + 8]
            high = line_x[t, 8 * r + 8 : 8 * r + 16]
            own_x[8 * r + 2 * t] = scale_x * jnp.where(first_lane, low, shift_lanes(high, 64))
            own_x[8 * r + 2 * t + 1] = scale_x * jnp.where(first_lane, shift_lanes(low, 64), high)
        for c in range(8):
            low = line_y[8 * c : 8 * c + 8]
            high = line_y[8 * c + 8 : 8 * c + 16]
            own_y[8 * r + c] = scale_y * jnp.where(
                lane < 4, shift_lanes(low, -4 * r), shift_lanes(high, 4 - 4 * r)
            )

    whole_copy(*box_args).wait_recv()
    for b in range(8):
        at = 8 * me + b
        device = tabs[T_DEV, at] & 15
        local = tabs[T_LOC, at] & 7
        owner = tabs[T_OWN, at] & 15
        second = tabs[T_RANK, at] == 1
        stays = device == me
        for f in range(5):
            box = jnp.where(stays, boxes[local, f], box_recv[device, 8 * f : 8 * f + 8])
            mixed[f, 16 * b + 8 : 16 * b + 16] = box
            own = box_recv[owner, 40 + 2 * f : 42 + 2 * f]
            mixed[f, 16 * b + 6 : 16 * b + 8] = jnp.where(second, pltpu.roll(own, 64, axis=1), own)
    whole_copy(*ghost_args).wait_recv()
    side_parts = [jnp.zeros((8, 128), F32) for _ in range(5)]
    for b in range(8):
        at = 8 * me + b
        owner = tabs[T_OWN, at] & 15
        second = tabs[T_RANK, at] == 1
        for f in range(5):
            inner = ghost_recv[owner, 6 * f : 6 * f + 8]
            mixed[f, 16 * b : 16 * b + 6] = jnp.where(second, shift_lanes(inner, 64), inner)[0:6]
        column = tabs[T_SPOT, at] & 7
        low_edge = ghost_recv[(owner + 15) & 15, 38:46]
        high_edge = ghost_recv[(owner + 1) & 15, 36:44]
        side = ghost_recv[owner, 30:38]
        side = jnp.where((sub < 3) & (column == 0), low_edge, side)
        side = jnp.where((sub >= 5) & (column == 7), high_edge, side)
        side = jnp.where(second, shift_lanes(side, -50), side)
        for f in range(5):
            side_parts[f] = jnp.where((lane >> 4) == b, shift_lanes(side, 16 * b - 10 * f), side_parts[f])

    ring = (lane - 4) & 127
    row = ring & 15
    base = ring - row
    coarse_row = (row >> 1) + 1

    def kept(i):
        return jnp.where(i < 3, i, jnp.where(i < 6, 6, jnp.where(i == 6, 7, i - 4)))

    inner_index = [base + kept(coarse_row + d) for d in (0, -1, 1)]
    side_rows = [base + coarse_row + d for d in (0, -1, 1)]
    interior = (lane & 8) != 0
    row_sign = jnp.where((row & 1) == 0, -0.25, 0.25)
    for f in range(5):
        turned[f] = mixed[f].T
        for k in range(8):
            block = turned[f, 8 * k : 8 * k + 8]
            mid, low, high = [pick_lanes(block, index) for index in inner_index]
            coarse_c[f, 3 + 8 * k : 11 + 8 * k] = mid
            coarse_s[f, 3 + 8 * k : 11 + 8 * k] = row_sign * minmod(mid - low, high - mid)
        mid, low, high = [pick_lanes(side_parts[f], index) for index in side_rows]
        slope = row_sign * minmod(mid - low, high - mid)
        coarse_c[f, 0:4] = mid[0:4]
        coarse_c[f, 66:70] = mid[4:8]
        coarse_s[f, 0:4] = slope[0:4]
        coarse_s[f, 66:70] = slope[4:8]
        for k in range(9):
            j = 1 + 8 * k
            mid = coarse_c[f, j : j + 8]
            slope = minmod(mid - coarse_c[f, j - 1 : j + 7], coarse_c[f, j + 1 : j + 9] - mid)
            middle = mid + coarse_s[f, j : j + 8]
            state_a[f, pl.ds(2 * j - 2, 8, stride=2), :] = middle - 0.25 * slope
            state_a[f, pl.ds(2 * j - 1, 8, stride=2), :] = middle + 0.25 * slope
        for k in range(16):
            m = 4 + 8 * k
            state_a[f, m : m + 8] = jnp.where(interior, turned[f, 8 * k : 8 * k + 8], state_a[f, m : m + 8])

    lower_face = (lane & 15) == 7

    def y_sides(state, m):
        lower, upper = cell_sides(
            [state[f, m : m + 8] for f in range(5)],
            [state[f, m + 1 : m + 9] for f in range(5)],
            [state[f, m + 2 : m + 10] for f in range(5)],
            2,
        )
        for f in range(5):
            low_y[f, m + 9 : m + 17] = lower[f]
            high_y[f, m + 9 : m + 17] = upper[f]

    def y_change(f, m):
        after = high_y[f, m + 8 : m + 16] + low_y[f, m + 9 : m + 17]
        before = high_y[f, m + 7 : m + 15] + low_y[f, m + 8 : m + 16]
        return after - before

    def x_sides(state, m):
        cells = [state[f, m : m + 8] for f in range(5)]
        lower, upper = cell_sides(
            [shift_lanes(u, 1) for u in cells], cells, [shift_lanes(u, -1) for u in cells], 1
        )
        for f in range(5):
            low_x[f, m : m + 8] = lower[f]
            high_x[f, m : m + 8] = upper[f]

    def x_fluxes(f, m):
        lower = low_x[f, m : m + 8]
        upper = high_x[f, m : m + 8]
        return upper + shift_lanes(lower, -1), shift_lanes(upper, 1) + lower

    def y_faces(add):
        for f in range(5):
            for i, m in enumerate((3, 131)):
                flux = high_y[f, m + 8 : m + 9] + low_y[f, m + 9 : m + 10]
                faces_y[i, f : f + 1] = faces_y[i, f : f + 1] + flux if add else flux

    def first_step(m):
        for f in range(5):
            after, before = x_fluxes(f, m)
            faces_x[f, m : m + 8] = jnp.where(lower_face, after, before)
            state_b[f, m : m + 8] = state_a[f, m : m + 8] - HALF_STEP * ((after - before) + y_change(f, m))

    for m in range(0, 136, 8):
        y_sides(state_a, m)
        x_sides(state_a, m)
    for m in range(0, 136, 8):
        first_step(m)
    y_faces(False)

    def second_step_x(m):
        for f in range(5):
            after, before = x_fluxes(f, m)
            faces_x[f, m : m + 8] = faces_x[f, m : m + 8] + jnp.where(lower_face, after, before)
            change_x[f, m : m + 8] = after - before

    for m in range(0, 136, 8):
        x_sides(state_b, m)
    for m in range(0, 136, 8):
        second_step_x(m)
    y_sides(state_b, 0)
    y_sides(state_b, 128)
    y_faces(True)
    box_lane = 16 * (lane & 7)
    face_index = jnp.where((lane & 8) == 0, box_lane + 7, (box_lane + 16) & 127)
    for k in range(8):
        m = 4 + 16 * k
        block = jnp.zeros((8, 128), F32)
        for f in range(5):
            pairs = faces_x[f, pl.ds(m, 8, stride=2), :] + faces_x[f, pl.ds(m + 1, 8, stride=2), :]
            block = jnp.where((lane >> 4) == f, pick_lanes(pairs, face_index), block)
        face_cols[8 * k : 8 * k + 8] = block
    face_rows[...] = face_cols[...].T
    for f in range(5):
        low = face_rows[16 * f : 16 * f + 8]
        high = face_rows[16 * f + 8 : 16 * f + 16]
        sums_x[pl.ds(f, 8, stride=8), :] = jnp.where(first_lane, low, shift_lanes(high, 64))
    low = faces_y[0] + shift_lanes(faces_y[0], -1)
    high = faces_y[1] + shift_lanes(faces_y[1], -1)
    field = jnp.where(lane < 40, lane >> 3, (lane >> 3) - 5)
    for b in range(8):
        index = 16 * b + 8 + 2 * (lane & 3)
        both = jnp.where((lane & 4) == 0, pick_lanes(low, index), pick_lanes(high, index))
        sums_y[b : b + 1] = jnp.sum(jnp.where(sub == field, both, 0.0), axis=0, keepdims=True)

    def pack_sums(o, dest, slot):
        at = 8 * peer(o)
        first = tabs[T_BACK, at] & 7
        second = tabs[T_BACK + 1, at] & 7
        dest[slot, 0:8] = sums_x[pl.ds(8 * first, 8), :]
        dest[slot, 5:13] = sums_x[pl.ds(8 * second, 8), :]
        dest[slot, 10:11] = jnp.where(lane[0:1] < 40, sums_y[pl.ds(first, 1)], sums_y[pl.ds(second, 1)])

    def send_sums(o, carry):
        pack_sums(o, sum_send, o)
        group_copy(*sum_args, o).start()
        return carry

    lax.fori_loop(1, GROUP, send_sums, 0)
    pack_sums(0, sum_recv, me)

    for m in range(8, 128, 8):
        y_sides(state_b, m)
    for m in range(0, 136, 8):
        for f in range(5):
            state_a[f, m : m + 8] = state_b[f, m : m + 8] - HALF_STEP * (change_x[f, m : m + 8] + y_change(f, m))
    for f in range(5):
        back[f] = state_a[f, 4:132].T
        for b in range(8):
            fine_out[b, f] = back[f, 16 * b + 8 : 16 * b + 16]

    both_halos.wait_send()
    both_edges.wait_send()
    whole_copy(*box_args).wait_send()
    whole_copy(*ghost_args).wait_send()
    whole_copy(*sum_args).wait_recv()

    sign_x = jnp.where(first_lane, SUM_SCALE, -SUM_SCALE)
    sign_y = jnp.where(lane < 4, SUM_SCALE, -SUM_SCALE)
    y_index = 8 * jnp.minimum(sub, 4) + (lane & 7)
    for n in range(32):
        entry = tabs[T_INV, n]
        live = entry > 0
        slot = (entry - 1) & 31
        sender = slot >> 1
        total_x = sum_recv[sender, pl.ds(5 * (slot & 1), 8), :]
        total_y = jnp.broadcast_to(sum_recv[sender, 10:11], (8, 128))
        total_y = pick_lanes(total_y, y_index + 40 * (slot & 1))
        out_x[pl.ds(n, 5, stride=32), :] = jnp.where(live, own_x[n, 0:5] - sign_x[0:5] * total_x[0:5], 0.0)
        out_y[pl.ds(n, 5, stride=32), :] = jnp.where(live, own_y[n, 0:5] - sign_y[0:5] * total_y[0:5], 0.0)
    for f in range(5):
        reflux_out[f, :, 0:128] = out_x[32 * f : 32 * f + 32]
        reflux_out[f, :, 128:136] = out_y[32 * f : 32 * f + 32][:, 0:8]

    whole_copy(*sum_args).wait_send()


def write_out(fine_in, reflux_in, fine_out, reflux_out, sems):
    copies = [
        pltpu.make_async_copy(fine_in, fine_out, sems.at[0]),
        pltpu.make_async_copy(reflux_in, reflux_out, sems.at[1]),
    ]
    for copy in copies:
        copy.start()
    for copy in copies:
        copy.wait()


def local(previous_fine_boxes, coarse_state, new_source, box_position):
    vmem = pl.BlockSpec(memory_space=pltpu.VMEM)
    hbm = pl.BlockSpec(memory_space=pltpu.HBM)
    dma = pltpu.SemaphoreType.DMA
    v = pltpu.VMEM
    fine, reflux = pl.pallas_call(
        body,
        out_shape=(
            jax.ShapeDtypeStruct((8, 5, 8, 128), F32),
            jax.ShapeDtypeStruct((5, 32, 136), F32),
        ),
        in_specs=[hbm] * 3,
        out_specs=(vmem, vmem),
        scratch_shapes=[
            v((8, 5, 8, 128), F32),
            v((5, 16, 512), F32),
            v((2, 8, 128), I32),
            v((16, 128), I32),
            pltpu.SMEM((16, 128), I32),
            v((40, 48, 128), F32),
            v((4, 128, 128), F32),
            v((1040, 128), F32),
            v((2, 4, 16, 128), F32),
            v((2, 4, 16, 128), F32),
            v((2, 8, 128), F32),
            v((2, 8, 128), F32),
            v((16, 56, 128), F32),
            v((16, 56, 128), F32),
            v((16, 48, 128), F32),
            v((16, 48, 128), F32),
            v((16, 16, 128), F32),
            v((16, 16, 128), F32),
            v((5, 128, 128), F32),
            v((5, 128, 128), F32),
            v((5, 80, 128), F32),
            v((5, 80, 128), F32),
            v((5, 152, 128), F32),
            v((5, 152, 128), F32),
            v((5, 160, 128), F32),
            v((5, 160, 128), F32),
            v((5, 136, 128), F32),
            v((5, 136, 128), F32),
            v((5, 136, 128), F32),
            v((5, 152, 128), F32),
            v((2, 8, 128), F32),
            v((128, 128), F32),
            v((128, 128), F32),
            v((5, 128, 128), F32),
            v((72, 128), F32),
            v((8, 128), F32),
            v((4, 72, 128), F32),
            v((136, 128), F32),
            v((32, 8, 128), F32),
            v((32, 8, 128), F32),
            v((192, 128), F32),
            v((192, 128), F32),
            *[dma] * 14,
        ],
        compiler_params=pltpu.CompilerParams(
            collective_id=0, has_side_effects=True, vmem_limit_bytes=54880 * 1024
        ),
    )(
        previous_fine_boxes,
        coarse_state,
        jnp.stack([new_source.reshape(8, 128), box_position.reshape(8, 128)]),
    )
    fine, reflux = pl.pallas_call(
        write_out,
        out_shape=(
            jax.ShapeDtypeStruct((8, 5, 8, 128), F32),
            jax.ShapeDtypeStruct((5, 32, 136), F32),
        ),
        in_specs=[vmem] * 2,
        out_specs=(hbm, hbm),
        scratch_shapes=[dma((2,))],
        compiler_params=pltpu.CompilerParams(vmem_limit_bytes=1024 * 1024),
    )(fine, reflux)
    return fine, jnp.transpose(reflux, (1, 0, 2))


def solution(mesh):
    placed = (P(("gx", "gy"), None, None, None), P(None, "gx", "gy"), P(), P())
    return jax.shard_map(
        local,
        mesh=mesh,
        in_specs=placed,
        out_specs=(P(("gx", "gy"), None, None, None), P(("gx", "gy"), None, None)),
        check_vma=False,
    )
```

```python
import jax
import jax.numpy as jnp
from jax import lax
from jax.experimental import pallas as pl
from jax.experimental.pallas import tpu as pltpu
from jax.sharding import PartitionSpec as P

MESH = pl.DeviceIdType.MESH
F32 = jnp.float32
I32 = jnp.int32

GROUP = 16
SLABS = 8
BOXES = 1024
GAMMA_LESS = 0.4
STEP_RATIO = 0.15
WAVE_SPEED = 2.5
HALF_STEP = 0.5 * STEP_RATIO
SUM_SCALE = 0.25 * STEP_RATIO * 0.5

T_DEV, T_LOC, T_OWN, T_RANK, T_SPOT, T_BOX, T_INV = 0, 1, 2, 3, 4, 5, 6
T_POS, T_POS_NEXT, T_POS_BEFORE, T_BACK = 8, 10, 12, 14


def iota(axis):
    return lax.broadcasted_iota(I32, (8, 128), axis)


def shift_lanes(x, by):
    by = by % 128
    return x if by == 0 else pltpu.roll(x, by, axis=1)


def pick_lanes(x, index):
    return jnp.take_along_axis(x, index, axis=1)


def minmod(a, b):
    return jnp.maximum(jnp.minimum(a, b), jnp.minimum(jnp.maximum(a, b), 0.0))


def scaled_flux(state, along, sign):
    rho, m1, m2, m3, energy = state
    speed = sign * WAVE_SPEED
    inverse = 1.0 / rho
    pressure = GAMMA_LESS * (energy - 0.5 * (m1 * m1 + m2 * m2 + m3 * m3) * inverse)
    normal = state[along] * inverse
    moved = normal + speed
    pieces = [
        state[along] + speed * rho, m1 * moved, m2 * moved, m3 * moved, energy * moved + pressure * normal
    ]
    pieces[along] = pieces[along] + pressure
    return pieces


def cell_sides(low, mid, high, along):
    half = [0.5 * minmod(m - l, h - m) for l, m, h in zip(low, mid, high)]
    lower = scaled_flux([m - s for m, s in zip(mid, half)], along, -1.0)
    upper = scaled_flux([m + s for m, s in zip(mid, half)], along, 1.0)
    return lower, upper


def interface_flux(cells, along):
    a, b, c, d = cells
    left = [y + 0.5 * minmod(y - x, z - y) for x, y, z in zip(a, b, c)]
    right = [y - 0.5 * minmod(y - x, z - y) for x, y, z in zip(b, c, d)]
    upper = scaled_flux(left, along, 1.0)
    lower = scaled_flux(right, along, -1.0)
    return [u + l for u, l in zip(upper, lower)]


def make_tables(maps, gx, me, table):
    lane = iota(1)
    sub = iota(0)
    both = jnp.broadcast_to(maps[pl.ds(gx, 1), :], (8, 128))
    src = both & 127
    pos = (both >> 10) & 511
    place = pick_lanes(pos, src)
    device = src >> 3
    local = src & 7
    owner = place >> 5
    spot = place & 31
    within = lane & 7
    group = lane >> 3
    rank = jnp.zeros((8, 128), I32)
    for d in range(1, 8):
        rank = rank + jnp.where((within >= d) & (shift_lanes(owner, d) == owner), 1, 0)

    def group_sum(v):
        for d in (1, 2, 4):
            v = v + shift_lanes(v, -d)
        return v

    mine = 8 * me + within
    my_owner = pick_lanes(owner, mine)
    my_rank = pick_lanes(rank, mine)
    after = (me + 1) & 15
    before = (me + 15) & 15
    rows = [device, local, owner, rank, spot, group_sum(jnp.where(device == me, local, 0)) & 7]
    inverse = jnp.zeros((8, 128), I32)
    for block in range(4):
        number = sub + 8 * block
        v = jnp.where((owner == me) & (spot == number), group * 2 + rank + 1, 0)
        for d in (64, 32, 16, 8, 4, 2, 1):
            v = v + shift_lanes(v, d)
        inverse = inverse + jnp.where(lane == number, v, 0)
    for d in (4, 2, 1):
        inverse = inverse + pltpu.roll(inverse, d, axis=0)
    rows += [jnp.minimum(inverse, 32), rank]
    for whose in (me, after, before):
        for a in range(2):
            rows.append(group_sum(jnp.where((owner == whose) & (rank == a), spot, 0)) & 31)
    for a in range(2):
        rows.append(group_sum(jnp.where((my_owner == group) & (my_rank == a), within, 0)) & 7)
    for i, row in enumerate(rows):
        table[pl.ds(i, 1), :] = row[0:1, :]


def body(
    boxes_in, coarse_in, maps_in, fine_out, reflux_out,
    boxes, coarse, maps, table, tabs, rim, rows_x, cols_x, halo_send, halo_recv, edge_send, edge_recv,
    box_send, box_recv, ghost_send, ghost_recv, sum_send, sum_recv,
    mixed, turned, coarse_c, coarse_s, state_a, state_b, low_y, high_y, low_x, high_x, change_x, faces_x, faces_y,
    face_cols, face_rows, back, sums_x, sums_y, line_x, line_y, own_x, own_y, out_x, out_y,
    table_sem, coarse_sem, maps_sem, boxes_sem, halo_ss, halo_rs, edge_ss, edge_rs,
    box_ss, box_rs, ghost_ss, ghost_rs, sum_ss, sum_rs,
):
    gx = lax.axis_index("gx")
    me = lax.axis_index("gy")
    lane = iota(1)
    sub = iota(0)

    def peer(o):
        return lax.rem(me + o, GROUP)

    def slab(o):
        return lax.rem(gx + o + SLABS, SLABS)

    near = [(slab(1), me), (slab(-1), me)]
    beside = [(gx, peer(GROUP - 1)), (gx, peer(1))]
    barrier = pltpu.get_barrier_semaphore()
    for there in near:
        pl.semaphore_signal(barrier, inc=1, device_id=there, device_id_type=MESH)
    for o in (1, 15, 4, 12, 2, 14, 8, 3, 13, 5, 11, 6, 10, 7, 9):
        pl.semaphore_signal(barrier, inc=1, device_id=(gx, peer(o)), device_id_type=MESH)
    fetches = [
        pltpu.make_async_copy(coarse_in, coarse, coarse_sem),
        pltpu.make_async_copy(maps_in, maps, maps_sem),
        pltpu.make_async_copy(boxes_in, boxes, boxes_sem),
    ]
    for fetch in fetches:
        fetch.start()

    fetches[1].wait()
    make_tables(maps, gx, me, table)
    to_scalars = pltpu.make_async_copy(table, tabs, table_sem)
    to_scalars.start()

    fetches[0].wait()
    for t in range(4):
        for f in range(5):
            tile = coarse[f, :, t * 128 : t * 128 + 128]
            halo_send[0, t, 3 * f : 3 * f + 3] = tile[13:16]
            halo_send[1, t, 3 * f : 3 * f + 3] = tile[0:3]
            rim[t * 5 + f, 8:24] = tile
            rim[20 + t * 5 + f, 8:24] = pltpu.roll(tile, 64, axis=1)
            rows_x[t, 22 * f + 3 : 22 * f + 19] = tile

    pl.semaphore_wait(barrier, GROUP + 1)
    def halo_copy(part, there):
        return pltpu.make_async_remote_copy(
            halo_send.at[part], halo_recv.at[part], halo_ss, halo_rs, there, MESH
        )

    for i, there in enumerate(near):
        halo_copy(i, there).start()
    both_halos = halo_copy(pl.ds(0, 2), near[0])

    to_scalars.wait()
    fetches[2].wait()

    def group_copy(source, target, rows, sems, o):
        return pltpu.make_async_remote_copy(
            source.at[o, pl.ds(0, rows)], target.at[me, pl.ds(0, rows)], *sems, (gx, peer(o)), MESH
        )

    def whole_copy(source, target, rows, sems):
        parts = (pl.ds(0, GROUP - 1), pl.ds(0, rows))
        return pltpu.make_async_remote_copy(source.at[parts], target.at[parts], *sems, (gx, peer(1)), MESH)

    box_args = (box_send, box_recv, 50, (box_ss, box_rs))
    ghost_args = (ghost_send, ghost_recv, 44, (ghost_ss, ghost_rs))
    sum_args = (sum_send, sum_recv, 11, (sum_ss, sum_rs))

    first_lane = lane < 64

    def patches(at):
        spots = [tabs[T_POS, at] & 31, tabs[T_POS + 1, at] & 31]
        rs = [s >> 3 for s in spots]
        cs = [s & 7 for s in spots]
        ids = [(((c & 1) ^ a) * 4 + (c >> 1)) * 5 for a, c in enumerate(cs)]
        return rs, cs, ids

    def pack_own(at, dest, slot):
        rs, _, ids = patches(at)
        for f in range(5):
            parts = [
                jnp.where(
                    sub == 0, rim[ids[a] + f, pl.ds(4 * rs[a] + 8, 8), :], rim[ids[a] + f, pl.ds(4 * rs[a] + 10, 8), :]
                )
                for a in range(2)
            ]
            dest[slot, 40 + 2 * f : 42 + 2 * f] = jnp.where(first_lane, parts[0], parts[1])[0:2]

    def send_box(o, carry):
        at = 8 * peer(o)
        which = tabs[T_BOX, at] & 7
        for f in range(5):
            box_send[o, 8 * f : 8 * f + 8] = boxes[which, f]
        pack_own(at, box_send, o)
        group_copy(*box_args, o).start()
        return carry

    lax.fori_loop(1, GROUP, send_box, 0)
    pack_own(8 * me, box_recv, me)

    both_halos.wait_recv()
    for t in range(4):
        for f in range(5):
            top = halo_recv[0, t, 3 * f : 3 * f + 3]
            bottom = halo_recv[1, t, 3 * f : 3 * f + 3]
            rim[t * 5 + f, 5:8] = top
            rim[t * 5 + f, 24:27] = bottom
            rim[20 + t * 5 + f, 5:8] = pltpu.roll(top, 64, axis=1)
            rim[20 + t * 5 + f, 24:27] = pltpu.roll(bottom, 64, axis=1)
            rows_x[t, 22 * f : 22 * f + 3] = top
            rows_x[t, 22 * f + 19 : 22 * f + 22] = bottom
    for t in range(4):
        cols_x[8 + 128 * t : 136 + 128 * t] = rows_x[t].T
    def edge_copy(part, there):
        return pltpu.make_async_remote_copy(
            edge_send.at[part], edge_recv.at[part], edge_ss, edge_rs, there, MESH
        )

    for i, (at, there) in enumerate(zip((8, 512), beside)):
        edge_send[i] = cols_x[at : at + 8]
        edge_copy(i, there).start()
    both_edges = edge_copy(pl.ds(0, 2), beside[0])

    top_rows = sub < 4
    tenth = jnp.zeros((8, 128), I32)
    for i in range(1, 12):
        tenth = tenth + jnp.where(lane >= 10 * i, 1, 0)
    side_index = jnp.where(lane < 100, 22 * jnp.where(tenth >= 5, tenth - 5, tenth) + lane - 10 * tenth, 0)

    def pack_ghosts(o, dest, slot):
        at = 8 * peer(o)
        rs, cs, ids = patches(at)
        for f in range(5):
            parts = [
                jnp.where(
                    sub < 3, rim[ids[a] + f, pl.ds(4 * rs[a] + 5, 8), :], rim[ids[a] + f, pl.ds(4 * rs[a] + 9, 8), :]
                )
                for a in range(2)
            ]
            dest[slot, 6 * f : 6 * f + 6] = jnp.where(first_lane, parts[0], parts[1])[0:6]
        sides = []
        for a in range(2):
            strip = jnp.where(
                top_rows, cols_x[pl.ds(64 * cs[a] + 5, 8), :], cols_x[pl.ds(64 * cs[a] + 67, 8), :]
            )
            sides.append(pick_lanes(strip, side_index + 4 * rs[a]))
        dest[slot, 30:38] = jnp.where(lane < 50, sides[0], sides[1])
        edge = jnp.where(sub < 3, cols_x[517:525], cols_x[5:13])
        edges = []
        for a in range(2):
            low = (tabs[T_POS_NEXT + a, at] & 31) >> 3
            high = (tabs[T_POS_BEFORE + a, at] & 31) >> 3
            edges.append(pick_lanes(edge, side_index + 4 * jnp.where(sub < 3, low, high)))
        dest[slot, 38:44] = jnp.where(lane < 50, edges[0], edges[1])[0:6]

    def send_ghosts(o, carry):
        pack_ghosts(o, ghost_send, o)
        group_copy(*ghost_args, o).start()
        return carry

    lax.fori_loop(1, GROUP, send_ghosts, 0)
    pack_ghosts(0, ghost_recv, me)

    scale_x = jnp.where(first_lane, HALF_STEP, -HALF_STEP)
    for t in range(4):
        cells = [
            [rim[t * 5 + f, pl.ds(8 + k, 8, stride=4), :] for f in range(5)] for k in (-2, -1, 0, 1)
        ]
        flux = interface_flux(cells, 1)
        for f in range(5):
            line_x[t, pl.ds(f, 8, stride=8), :] = flux[f]
    both_edges.wait_recv()
    cols_x[0:8] = edge_recv[1]
    cols_x[520:528] = edge_recv[0]
    for f5 in range(2):
        cells = [
            [
                shift_lanes(cols_x[pl.ds(8 + k + 512 * f5, 8, stride=64), :], -(22 * f + 3))
                for f in range(5)
            ]
            for k in (-2, -1, 0, 1)
        ]
        flux = interface_flux(cells, 2)
        for f in range(5):
            line_y[pl.ds(64 * f5 + f, 8, stride=8), :] = flux[f]
    scale_y = jnp.where(lane < 4, HALF_STEP, -HALF_STEP)
    for r in range(4):
        for t in range(4):
            low = line_x[t, 8 * r : 8 * r + 8]
            high = line_x[t, 8 * r + 8 : 8 * r + 16]
            own_x[8 * r + 2 * t] = scale_x * jnp.where(first_lane, low, shift_lanes(high, 64))
            own_x[8 * r + 2 * t + 1] = scale_x * jnp.where(first_lane, shift_lanes(low, 64), high)
        for c in range(8):
            low = line_y[8 * c : 8 * c + 8]
            high = line_y[8 * c + 8 : 8 * c + 16]
            own_y[8 * r + c] = scale_y * jnp.where(
                lane < 4, shift_lanes(low, -4 * r), shift_lanes(high, 4 - 4 * r)
            )

    whole_copy(*box_args).wait_recv()
    for b in range(8):
        at = 8 * me + b
        device = tabs[T_DEV, at] & 15
        local = tabs[T_LOC, at] & 7
        owner = tabs[T_OWN, at] & 15
        second = tabs[T_RANK, at] == 1
        stays = device == me
        for f in range(5):
            box = jnp.where(stays, boxes[local, f], box_recv[device, 8 * f : 8 * f + 8])
            mixed[f, 16 * b + 8 : 16 * b + 16] = box
            own = box_recv[owner, 40 + 2 * f : 42 + 2 * f]
            mixed[f, 16 * b + 6 : 16 * b + 8] = jnp.where(second, pltpu.roll(own, 64, axis=1), own)
    whole_copy(*ghost_args).wait_recv()
    side_parts = [jnp.zeros((8, 128), F32) for _ in range(5)]
    for b in range(8):
        at = 8 * me + b
        owner = tabs[T_OWN, at] & 15
        second = tabs[T_RANK, at] == 1
        for f in range(5):
            inner = ghost_recv[owner, 6 * f : 6 * f + 8]
            mixed[f, 16 * b : 16 * b + 6] = jnp.where(second, shift_lanes(inner, 64), inner)[0:6]
        column = tabs[T_SPOT, at] & 7
        low_edge = ghost_recv[(owner + 15) & 15, 38:46]
        high_edge = ghost_recv[(owner + 1) & 15, 36:44]
        side = ghost_recv[owner, 30:38]
        side = jnp.where((sub < 3) & (column == 0), low_edge, side)
        side = jnp.where((sub >= 5) & (column == 7), high_edge, side)
        side = jnp.where(second, shift_lanes(side, -50), side)
        for f in range(5):
            side_parts[f] = jnp.where((lane >> 4) == b, shift_lanes(side, 16 * b - 10 * f), side_parts[f])

    ring = (lane - 4) & 127
    row = ring & 15
    base = ring - row
    coarse_row = (row >> 1) + 1

    def kept(i):
        return jnp.where(i < 3, i, jnp.where(i < 6, 6, jnp.where(i == 6, 7, i - 4)))

    inner_index = [base + kept(coarse_row + d) for d in (0, -1, 1)]
    side_rows = [base + coarse_row + d for d in (0, -1, 1)]
    interior = (lane & 8) != 0
    row_sign = jnp.where((row & 1) == 0, -0.25, 0.25)
    for f in range(5):
        turned[f] = mixed[f].T
        for k in range(8):
            block = turned[f, 8 * k : 8 * k + 8]
            mid, low, high = [pick_lanes(block, index) for index in inner_index]
            coarse_c[f, 3 + 8 * k : 11 + 8 * k] = mid
            coarse_s[f, 3 + 8 * k : 11 + 8 * k] = row_sign * minmod(mid - low, high - mid)
        mid, low, high = [pick_lanes(side_parts[f], index) for index in side_rows]
        slope = row_sign * minmod(mid - low, high - mid)
        coarse_c[f, 0:4] = mid[0:4]
        coarse_c[f, 66:70] = mid[4:8]
        coarse_s[f, 0:4] = slope[0:4]
        coarse_s[f, 66:70] = slope[4:8]
        for k in range(9):
            j = 1 + 8 * k
            mid = coarse_c[f, j : j + 8]
            slope = minmod(mid - coarse_c[f, j - 1 : j + 7], coarse_c[f, j + 1 : j + 9] - mid)
            middle = mid + coarse_s[f, j : j + 8]
            state_a[f, pl.ds(2 * j - 2, 8, stride=2), :] = middle - 0.25 * slope
            state_a[f, pl.ds(2 * j - 1, 8, stride=2), :] = middle + 0.25 * slope
        for k in range(16):
            m = 4 + 8 * k
            state_a[f, m : m + 8] = jnp.where(interior, turned[f, 8 * k : 8 * k + 8], state_a[f, m : m + 8])

    lower_face = (lane & 15) == 7

    def y_sides(state, m):
        lower, upper = cell_sides(
            [state[f, m : m + 8] for f in range(5)],
            [state[f, m + 1 : m + 9] for f in range(5)],
            [state[f, m + 2 : m + 10] for f in range(5)],
            2,
        )
        for f in range(5):
            low_y[f, m + 9 : m + 17] = lower[f]
            high_y[f, m + 9 : m + 17] = upper[f]

    def y_change(f, m):
        after = high_y[f, m + 8 : m + 16] + low_y[f, m + 9 : m + 17]
        before = high_y[f, m + 7 : m + 15] + low_y[f, m + 8 : m + 16]
        return after - before

    def x_sides(state, m):
        cells = [state[f, m : m + 8] for f in range(5)]
        lower, upper = cell_sides(
            [shift_lanes(u, 1) for u in cells], cells, [shift_lanes(u, -1) for u in cells], 1
        )
        for f in range(5):
            low_x[f, m : m + 8] = lower[f]
            high_x[f, m : m + 8] = upper[f]

    def x_fluxes(f, m):
        lower = low_x[f, m : m + 8]
        upper = high_x[f, m : m + 8]
        return upper + shift_lanes(lower, -1), shift_lanes(upper, 1) + lower

    def y_faces(add):
        for f in range(5):
            for i, m in enumerate((3, 131)):
                flux = high_y[f, m + 8 : m + 9] + low_y[f, m + 9 : m + 10]
                faces_y[i, f : f + 1] = faces_y[i, f : f + 1] + flux if add else flux

    def first_step(m):
        for f in range(5):
            after, before = x_fluxes(f, m)
            faces_x[f, m : m + 8] = jnp.where(lower_face, after, before)
            state_b[f, m : m + 8] = state_a[f, m : m + 8] - HALF_STEP * ((after - before) + y_change(f, m))

    for m in range(0, 136, 8):
        y_sides(state_a, m)
        x_sides(state_a, m)
    for m in range(0, 136, 8):
        first_step(m)
    y_faces(False)

    def second_step_x(m):
        for f in range(5):
            after, before = x_fluxes(f, m)
            faces_x[f, m : m + 8] = faces_x[f, m : m + 8] + jnp.where(lower_face, after, before)
            change_x[f, m : m + 8] = after - before

    for m in range(0, 136, 8):
        x_sides(state_b, m)
    for m in range(0, 136, 8):
        second_step_x(m)
    y_sides(state_b, 0)
    y_sides(state_b, 128)
    y_faces(True)
    box_lane = 16 * (lane & 7)
    face_index = jnp.where((lane & 8) == 0, box_lane + 7, (box_lane + 16) & 127)
    for k in range(8):
        m = 4 + 16 * k
        block = jnp.zeros((8, 128), F32)
        for f in range(5):
            pairs = faces_x[f, pl.ds(m, 8, stride=2), :] + faces_x[f, pl.ds(m + 1, 8, stride=2), :]
            block = jnp.where((lane >> 4) == f, pick_lanes(pairs, face_index), block)
        face_cols[8 * k : 8 * k + 8] = block
    face_rows[...] = face_cols[...].T
    for f in range(5):
        low = face_rows[16 * f : 16 * f + 8]
        high = face_rows[16 * f + 8 : 16 * f + 16]
        sums_x[pl.ds(f, 8, stride=8), :] = jnp.where(first_lane, low, shift_lanes(high, 64))
    low = faces_y[0] + shift_lanes(faces_y[0], -1)
    high = faces_y[1] + shift_lanes(faces_y[1], -1)
    field = jnp.where(lane < 40, lane >> 3, (lane >> 3) - 5)
    for b in range(8):
        index = 16 * b + 8 + 2 * (lane & 3)
        both = jnp.where((lane & 4) == 0, pick_lanes(low, index), pick_lanes(high, index))
        sums_y[b : b + 1] = jnp.sum(jnp.where(sub == field, both, 0.0), axis=0, keepdims=True)

    def pack_sums(o, dest, slot):
        at = 8 * peer(o)
        first = tabs[T_BACK, at] & 7
        second = tabs[T_BACK + 1, at] & 7
        dest[slot, 0:8] = sums_x[pl.ds(8 * first, 8), :]
        dest[slot, 5:13] = sums_x[pl.ds(8 * second, 8), :]
        dest[slot, 10:11] = jnp.where(lane[0:1] < 40, sums_y[pl.ds(first, 1)], sums_y[pl.ds(second, 1)])

    def send_sums(o, carry):
        pack_sums(o, sum_send, o)
        group_copy(*sum_args, o).start()
        return carry

    lax.fori_loop(1, GROUP, send_sums, 0)
    pack_sums(0, sum_recv, me)

    for m in range(8, 128, 8):
        y_sides(state_b, m)
    for m in range(0, 136, 8):
        for f in range(5):
            state_a[f, m : m + 8] = state_b[f, m : m + 8] - HALF_STEP * (change_x[f, m : m + 8] + y_change(f, m))
    for f in range(5):
        back[f] = state_a[f, 4:132].T
        for b in range(8):
            fine_out[b, f] = back[f, 16 * b + 8 : 16 * b + 16]

    both_halos.wait_send()
    both_edges.wait_send()
    whole_copy(*box_args).wait_send()
    whole_copy(*ghost_args).wait_send()
    whole_copy(*sum_args).wait_recv()

    sign_x = jnp.where(first_lane, SUM_SCALE, -SUM_SCALE)
    sign_y = jnp.where(lane < 4, SUM_SCALE, -SUM_SCALE)
    y_index = 8 * jnp.minimum(sub, 4) + (lane & 7)
    for n in range(32):
        entry = tabs[T_INV, n]
        live = entry > 0
        slot = (entry - 1) & 31
        sender = slot >> 1
        total_x = sum_recv[sender, pl.ds(5 * (slot & 1), 8), :]
        total_y = jnp.broadcast_to(sum_recv[sender, 10:11], (8, 128))
        total_y = pick_lanes(total_y, y_index + 40 * (slot & 1))
        out_x[pl.ds(n, 5, stride=32), :] = jnp.where(live, own_x[n, 0:5] - sign_x[0:5] * total_x[0:5], 0.0)
        out_y[pl.ds(n, 5, stride=32), :] = jnp.where(live, own_y[n, 0:5] - sign_y[0:5] * total_y[0:5], 0.0)
    for f in range(5):
        reflux_out[f, :, 0:128] = out_x[32 * f : 32 * f + 32]
        reflux_out[f, :, 128:136] = out_y[32 * f : 32 * f + 32][:, 0:8]

    whole_copy(*sum_args).wait_send()


def write_out(fine_in, reflux_in, fine_out, reflux_out, sems):
    copies = [
        pltpu.make_async_copy(fine_in, fine_out, sems.at[0]),
        pltpu.make_async_copy(reflux_in, reflux_out, sems.at[1]),
    ]
    for copy in copies:
        copy.start()
    for copy in copies:
        copy.wait()


def local(previous_fine_boxes, coarse_state, new_source, box_position):
    vmem = pl.BlockSpec(memory_space=pltpu.VMEM)
    hbm = pl.BlockSpec(memory_space=pltpu.HBM)
    dma = pltpu.SemaphoreType.DMA
    v = pltpu.VMEM
    fine, reflux = pl.pallas_call(
        body,
        out_shape=(
            jax.ShapeDtypeStruct((8, 5, 8, 128), F32),
            jax.ShapeDtypeStruct((5, 32, 136), F32),
        ),
        in_specs=[hbm] * 3,
        out_specs=(vmem, vmem),
        scratch_shapes=[
            v((8, 5, 8, 128), F32),
            v((5, 16, 512), F32),
            v((8, 128), I32),
            v((16, 128), I32),
            pltpu.SMEM((16, 128), I32),
            v((40, 48, 128), F32),
            v((4, 128, 128), F32),
            v((1040, 128), F32),
            v((2, 4, 16, 128), F32),
            v((2, 4, 16, 128), F32),
            v((2, 8, 128), F32),
            v((2, 8, 128), F32),
            v((16, 56, 128), F32),
            v((16, 56, 128), F32),
            v((16, 48, 128), F32),
            v((16, 48, 128), F32),
            v((16, 16, 128), F32),
            v((16, 16, 128), F32),
            v((5, 128, 128), F32),
            v((5, 128, 128), F32),
            v((5, 80, 128), F32),
            v((5, 80, 128), F32),
            v((5, 152, 128), F32),
            v((5, 152, 128), F32),
            v((5, 160, 128), F32),
            v((5, 160, 128), F32),
            v((5, 136, 128), F32),
            v((5, 136, 128), F32),
            v((5, 136, 128), F32),
            v((5, 152, 128), F32),
            v((2, 8, 128), F32),
            v((128, 128), F32),
            v((128, 128), F32),
            v((5, 128, 128), F32),
            v((72, 128), F32),
            v((8, 128), F32),
            v((4, 72, 128), F32),
            v((136, 128), F32),
            v((32, 8, 128), F32),
            v((32, 8, 128), F32),
            v((192, 128), F32),
            v((192, 128), F32),
            *[dma] * 14,
        ],
        compiler_params=pltpu.CompilerParams(
            collective_id=0, has_side_effects=True, vmem_limit_bytes=54880 * 1024
        ),
    )(
        previous_fine_boxes,
        coarse_state,
        (new_source + BOXES * box_position).reshape(8, 128),
    )
    fine, reflux = pl.pallas_call(
        write_out,
        out_shape=(
            jax.ShapeDtypeStruct((8, 5, 8, 128), F32),
            jax.ShapeDtypeStruct((5, 32, 136), F32),
        ),
        in_specs=[vmem] * 2,
        out_specs=(hbm, hbm),
        scratch_shapes=[dma((2,))],
        compiler_params=pltpu.CompilerParams(vmem_limit_bytes=1024 * 1024),
    )(fine, reflux)
    return fine, jnp.transpose(reflux, (1, 0, 2))


def solution(mesh):
    placed = (P(("gx", "gy"), None, None, None), P(None, "gx", "gy"), P(), P())
    return jax.shard_map(
        local,
        mesh=mesh,
        in_specs=placed,
        out_specs=(P(("gx", "gy"), None, None, None), P(("gx", "gy"), None, None)),
        check_vma=False,
    )
```
